512 devices in a mesh: tm: 128 (over x_hi, z, y), row: 2 (over core), col: 2 (over x_lo).
Axes of the slice: x: 4 (x_hi: 2, x_lo: 2; x = x_hi * 2 + x_lo), y: 4, z: 16, core: 2. Of those that a mesh axis runs over, the one named last changes fastest.
Arguments:
- precision_diag: float32 [256, 512, 512], P('tm', 'row', 'col'), may hold values from -4 to 16, as said below
- precision_link: float32 [256, 512, 512], P('tm', 'row', 'col'), may hold values from -8 to 2
Outputs:
- pivots: float32 [256, 512, 512], P('tm', 'row', 'col')
- couplings: float32 [256, 512, 512], P('tm', 'row', 'col')
- log_variance: float32 [256, 512], P('tm', ('row', 'col'))
The draws below stay inside these ranges and needn't reach their ends.
Inputs may be any that keep to these rules, and one draw needn't show every extreme that they name: precision_diag and precision_link form a symmetric positive definite block-tridiagonal matrix as in the reference program.
All inputs are finite; a program needn't handle non-finite values.
Results may differ from the reference program's by a relative error of at most 0.0003.
Values sent between devices are 32-bit elements; how exact they have to be, the bound alone decides.
No kernel may reach another device: no remote copies, remote signals or barrier semaphores. Data moves between devices by JAX's collectives and lax.ppermute only.
A program may use at most 128 MiB of HBM per device.

```python
import math
import jax
import jax.numpy as jnp
from jax import lax

NS = 512
LEVELS = 4
NT = 256


def paired_product(left_stack, right_stack):
    return jnp.einsum('jki,jkl->jil', left_stack, right_stack, precision=lax.Precision.HIGHEST)


def build_precision(key):
    base_key = jax.random.fold_in(key, 11)
    subkeys = jax.random.split(base_key, 6)
    scales = jnp.exp(jax.random.uniform(subkeys[0], (NT, NS), jnp.float32, math.log(0.7), math.log(2.2)))
    identity = jnp.eye(NS, dtype=jnp.float32)
    roughness = jax.random.normal(subkeys[1], (NT, NS, NS), jnp.float32) * (0.5 / math.sqrt(NS))
    factor = jnp.triu(roughness, 1) + scales[:, :, None] * identity
    persistence = jax.random.uniform(subkeys[2], (NT,), jnp.float32, 0.985, 0.999)
    shocked = jax.random.uniform(subkeys[3], (NT,), jnp.float32) < 0.03
    persistence = jnp.where(shocked, 0.6, persistence)
    perturbation = jax.random.normal(subkeys[4], (NT, NS, NS), jnp.float32) * (0.1 / math.sqrt(NS))
    transfer = persistence[:, None, None] * (factor + perturbation)
    nugget = jnp.exp(jax.random.uniform(subkeys[5], (NT, NS), jnp.float32, math.log(0.0001), math.log(0.01))) * scales * scales
    next_factor = jnp.roll(factor, -1, axis=0)
    next_transfer = jnp.roll(transfer, -1, axis=0)
    present = (jnp.arange(NT) < NT - 1).astype(jnp.float32)[:, None, None]
    diagonal_blocks = paired_product(factor, factor) + present * paired_product(next_transfer, next_transfer) + nugget[:, :, None] * identity
    link_blocks = -paired_product(next_factor, next_transfer)
    return (diagonal_blocks, link_blocks)


def draw_precision_diag(key, part):
    return build_precision(key)[0]


def draw_precision_link(key, part):
    return build_precision(key)[1]


def setup_inputs(seed: int = 0) -> dict:
    key_list = jax.random.split(jax.random.key(seed), 3)
    precision_diag = draw_precision_diag(jax.random.fold_in(key_list[2], 71), 0)
    precision_link = draw_precision_link(jax.random.fold_in(key_list[2], 71), 0)
    return dict(precision_diag=precision_diag, precision_link=precision_link)


def product_tn(left_part, right_part):
    return jnp.einsum('ki,kl->il', left_part, right_part, precision=lax.Precision.HIGHEST)

def eliminate_block(pivot, below_link, above_link):
    node_count = pivot.shape[0]
    lower_factor = jnp.linalg.cholesky(pivot)
    right_side = jnp.concatenate([below_link, above_link.T, jnp.eye(node_count, dtype=pivot.dtype)], axis=1)
    solved = jax.scipy.linalg.solve_triangular(lower_factor, right_side, lower=True)
    lower_panel = solved[:, :node_count]
    upper_panel = solved[:, node_count:2 * node_count]
    inverse_part = solved[:, 2 * node_count:]
    log_part = jnp.log(jnp.sum(inverse_part * inverse_part, axis=0))
    return (log_part, product_tn(lower_panel, lower_panel), product_tn(upper_panel, upper_panel), -product_tn(upper_panel, lower_panel))

def final_block(pivot):
    node_count = pivot.shape[0]
    lower_factor = jnp.linalg.cholesky(pivot)
    inverse_part = jax.scipy.linalg.solve_triangular(lower_factor, jnp.eye(node_count, dtype=pivot.dtype), lower=True)
    return jnp.log(jnp.sum(inverse_part * inverse_part, axis=0))

def reference(precision_diag, precision_link):
    block_total = precision_diag.shape[0]
    node_count = precision_diag.shape[1]
    pivots = precision_diag
    links = precision_link.at[block_total - 1].set(jnp.zeros((node_count, node_count), precision_link.dtype))
    out_pivots = pivots
    out_links = links
    out_logs = jnp.zeros((block_total, node_count), precision_diag.dtype)
    for level_num in range(LEVELS):
        stride = 2 ** level_num
        removed = jnp.arange(stride, block_total, 2 * stride, dtype=jnp.int32)
        lower_ids = (removed - stride).astype(jnp.int32)
        upper_ids = (removed + stride).astype(jnp.int32)
        log_part, gram_down, gram_up, link_new = jax.vmap(eliminate_block)(pivots[removed], links[lower_ids], links[removed])
        out_pivots = out_pivots.at[removed].set(pivots[removed])
        out_links = out_links.at[removed].set(links[removed])
        out_logs = out_logs.at[removed].set(log_part)
        pivots = pivots.at[lower_ids].add(-gram_down)
        pivots = pivots.at[upper_ids].add(-gram_up, mode='drop')
        links = links.at[lower_ids].set(link_new)
    kept = jnp.arange(0, block_total, 2 ** LEVELS, dtype=jnp.int32)
    out_pivots = out_pivots.at[kept].set(pivots[kept])
    out_links = out_links.at[kept].set(links[kept])
    out_logs = out_logs.at[kept].set(jax.vmap(final_block)(pivots[kept]))
    return (out_pivots, out_links, out_logs)
```

```python
import functools

import jax
import jax.numpy as jnp
from jax import lax
from jax.experimental import pallas as pl
from jax.experimental.pallas import tpu as pltpu
from jax.sharding import PartitionSpec as P

LEVELS = 4
LEAF = 32
TILE = 128
BF16 = jnp.bfloat16
F32 = jnp.float32


def upper_blocks(count):
    return [(i, j) for i in range(count) for j in range(i, count)]


def split(x, terms):
    out = []
    for i in range(terms):
        head = x.astype(BF16)
        out.append(head)
        if i + 1 < terms:
            x = x - head.astype(F32)
    return out


PAIRS = {2: ((1, 0), (0, 1), (0, 0)), 3: ((2, 0), (0, 2), (1, 1), (1, 0), (0, 1), (0, 0))}


def dot_of(left, right, dims):
    terms = len(left)
    total = None
    for i, j in PAIRS[terms]:
        part = lax.dot_general(left[i], right[j], (dims, ((), ())), preferred_element_type=F32)
        total = part if total is None else total + part
    return total


def stacked_tn(left, right, terms):
    lefts, rights = split(left, terms), split(right, terms)
    order = PAIRS[terms]
    return lax.dot_general(
        jnp.concatenate([lefts[i] for i, _ in order], 0),
        jnp.concatenate([rights[j] for _, j in order], 0),
        (((0,), (0,)), ((), ())),
        preferred_element_type=F32,
    )


def eliminated_rows(rows, offset):
    count, width = rows.shape
    row_ids = lax.broadcasted_iota(jnp.int32, (count, width), 0)
    col_ids = lax.broadcasted_iota(jnp.int32, (count, width), 1)
    sub_ids = lax.broadcasted_iota(jnp.int32, (8, 128), 0)
    groups = count // 8
    columns = []
    for j in range(count):
        first = j // 8
        spread = jnp.broadcast_to(
            rows[8 * first :, offset + j : offset + j + 1], (count - 8 * first, 128)
        )
        columns.append([spread[8 * i : 8 * i + 8] for i in range(groups - first)])
    inside = (col_ids >= offset) & (col_ids < offset + count)
    start = jnp.where(inside, (col_ids == row_ids + offset).astype(F32), rows)
    natural = [start[8 * g : 8 * g + 8] for g in range(groups)]
    scales = [jnp.zeros((8, 128), F32) for _ in range(groups)]

    def wide(x):
        return jnp.concatenate([x] * (width // 128), 1)

    for k in range(count):
        g, s = k // 8, k % 8
        pivot = columns[k][0][s : s + 1]
        inverse = 1.0 / pivot
        scales[g] = jnp.where(sub_ids == s, lax.rsqrt(pivot), scales[g])
        factors = [c * inverse for c in columns[k]]
        factors[0] = jnp.where(sub_ids > s, factors[0], 0.0)
        for j in range(k + 1, count):
            first = j // 8
            entry = columns[k][first - g][j % 8 : j % 8 + 1]
            for i in range(groups - first):
                columns[j][i] = columns[j][i] - factors[first - g + i] * entry
        row = natural[g][s : s + 1]
        for i in range(g, groups):
            natural[i] = natural[i] - wide(factors[i - g]) * row
    return jnp.concatenate([wide(scales[g]) * natural[g] for g in range(groups)], 0)


def factor_body(w_ref):
    size = w_ref.shape[0]
    col_ids = lax.broadcasted_iota(jnp.int32, (1, size), 1)
    total = jnp.zeros((1, size), F32)
    for offset in range(0, size, LEAF):
        end = offset + LEAF
        rows = eliminated_rows(w_ref[offset:end, :], offset)
        final = jnp.where(col_ids < end, rows, 0.0)
        w_ref[offset:end, :] = final
        total = total + jnp.sum(final * final, axis=0, keepdims=True)
        if end < size:
            update = stacked_tn(rows[:, end:], rows, 3)
            old = jnp.where((col_ids >= offset) & (col_ids < end), 0.0, w_ref[end:, :])
            w_ref[end:, :] = old - update
    return total


def unpack(blocks_ref, w_ref):
    for b, (i, j) in enumerate(upper_blocks(w_ref.shape[0] // TILE)):
        w_ref[i * TILE : (i + 1) * TILE, j * TILE : (j + 1) * TILE] = blocks_ref[b]
        if i != j:
            w_ref[j * TILE : (j + 1) * TILE, i * TILE : (i + 1) * TILE] = jnp.zeros(
                (TILE, TILE), F32
            )


def factor0_kernel(diag_ref, w_ref, sums_ref):
    unpack(diag_ref, w_ref)
    sums_ref[...] = factor_body(w_ref)


def factor_kernel(flag_ref, diag_ref, near_ref, far_ref, new_ref, w_ref, sums_ref):
    new_ref[...] = diag_ref[...] - near_ref[...] - far_ref[...]

    @pl.when(flag_ref[0] != 0)
    def _():
        unpack(new_ref, w_ref)
        sums_ref[...] = factor_body(w_ref)


def panel_kernel(flag_ref, w_ref, x_ref, y_ref, gram_ref):
    @pl.when(flag_ref[0] != 0)
    def _():
        size = w_ref.shape[0]
        x_parts = split(x_ref[...], 3)
        for i in range(size // TILE):
            end = (i + 1) * TILE
            w_parts = split(w_ref[i * TILE : end, :end], 3)
            y_ref[i * TILE : end, :] = dot_of(
                w_parts, [p[:end] for p in x_parts], ((1,), (0,))
            )
        y_parts = split(y_ref[...], 3)
        block = 0
        for i in range(size // TILE):
            left = [p[:, i * TILE : (i + 1) * TILE] for p in y_parts]
            strip = dot_of(left, [p[:, i * TILE :] for p in y_parts], ((0,), (0,)))
            for j in range(i, size // TILE):
                gram_ref[block] = strip[:, (j - i) * TILE : (j - i + 1) * TILE]
                block += 1

    @pl.when(flag_ref[0] == 0)
    def _():
        y_ref[...] = jnp.zeros_like(y_ref)
        gram_ref[...] = jnp.zeros_like(gram_ref)


def link_kernel(flag_ref, other_ref, y_ref, new_ref):
    @pl.when(flag_ref[0] != 0)
    def _():
        size = y_ref.shape[0]
        y_parts = split(y_ref[...], 3)
        other_parts = split(other_ref[...], 3)
        for i in range(size // TILE):
            left = [p[:, i * TILE : (i + 1) * TILE] for p in other_parts]
            new_ref[i * TILE : (i + 1) * TILE, :] = -dot_of(left, y_parts, ((0,), (0,)))

    @pl.when(flag_ref[0] == 0)
    def _():
        new_ref[...] = jnp.zeros_like(new_ref)


SMEM = pl.BlockSpec(memory_space=pltpu.SMEM)
VMEM = pl.BlockSpec(memory_space=pltpu.VMEM)
PARAMS = pltpu.CompilerParams(vmem_limit_bytes=48 * 1024 * 1024)


def factor(flag, diag, near, far, size):
    return pl.pallas_call(
        factor_kernel,
        out_shape=(
            jax.ShapeDtypeStruct(diag.shape, F32),
            jax.ShapeDtypeStruct((size, size), F32),
            jax.ShapeDtypeStruct((1, size), F32),
        ),
        in_specs=[SMEM, VMEM, VMEM, VMEM],
        out_specs=(VMEM, VMEM, VMEM),
        compiler_params=PARAMS,
        cost_estimate=pl.CostEstimate(flops=10**10, bytes_accessed=4 * 2**20, transcendentals=0),
    )(flag, diag, near, far)


def factor0(diag, size):
    return pl.pallas_call(
        factor0_kernel,
        out_shape=(
            jax.ShapeDtypeStruct((size, size), F32),
            jax.ShapeDtypeStruct((1, size), F32),
        ),
        in_specs=[VMEM],
        out_specs=(VMEM, VMEM),
        compiler_params=PARAMS,
        cost_estimate=pl.CostEstimate(flops=10**10, bytes_accessed=2 * 2**20, transcendentals=0),
    )(diag)


def panel(flag, w, x):
    size = w.shape[0]
    blocks = len(upper_blocks(size // TILE))
    return pl.pallas_call(
        panel_kernel,
        out_shape=(
            jax.ShapeDtypeStruct((size, size), F32),
            jax.ShapeDtypeStruct((blocks, TILE, TILE), F32),
        ),
        in_specs=[SMEM, VMEM, VMEM],
        out_specs=(VMEM, VMEM),
        compiler_params=PARAMS,
        cost_estimate=pl.CostEstimate(flops=3 * 10**9, bytes_accessed=4 * 2**20, transcendentals=0),
    )(flag, w, x)


def link(flag, other, y):
    return pl.pallas_call(
        link_kernel,
        out_shape=jax.ShapeDtypeStruct(y.shape, F32),
        in_specs=[SMEM, VMEM, VMEM],
        out_specs=VMEM,
        compiler_params=PARAMS,
        cost_estimate=pl.CostEstimate(flops=2 * 10**9, bytes_accessed=3 * 2**20, transcendentals=0),
    )(flag, other, y)


def swap_cores(x):
    return lax.ppermute(x, "row", [(0, 1), (1, 0)])


def swap_chips(x):
    return lax.ppermute(x, "col", [(0, 1), (1, 0)])


def gather_upper(tile, row_id, col_id):
    crossed = lax.ppermute(tile, ("row", "col"), [(0, 1), (3, 2)])
    mine = jnp.stack([tile, crossed])
    got = swap_cores(mine)
    core0 = jnp.where(row_id == 0, mine, got)
    core1 = jnp.where(row_id == 0, got, mine)
    first = jnp.where(col_id == 0, core0[0], core0[1])
    off = jnp.where(col_id == 0, core1[0].T, core0[0])
    last = jnp.where(col_id == 0, core1[1], core1[0])
    return first, off, last


def packed(first, off, last):
    half = first.shape[0]
    per = half // TILE

    def block(i, j):
        source = first if j < per else (off if i < per else last)
        i, j = i % per, j % per
        return source[i * TILE : (i + 1) * TILE, j * TILE : (j + 1) * TILE]

    return jnp.stack([block(i, j) for i, j in upper_blocks(2 * per)])


def own_tile(blocks, row_id, col_id, half):
    per = half // TILE
    at = {ij: b for b, ij in enumerate(upper_blocks(2 * per))}

    def block(i, j):
        return blocks[at[i, j]] if i <= j else blocks[at[j, i]].T

    def tile(r, c):
        return jnp.block(
            [[block(r * per + i, c * per + j) for j in range(per)] for i in range(per)]
        )

    off = tile(0, 1)
    return jnp.where(
        row_id == col_id,
        jnp.where(row_id == 0, tile(0, 0), tile(1, 1)),
        jnp.where(row_id == 0, off, off.T),
    )


def shards(precision_diag, precision_link):
    row_id = lax.axis_index("row")
    col_id = lax.axis_index("col")
    time_id = lax.axis_index("tm")
    groups = lax.axis_size("tm")
    half = precision_diag.shape[1]
    size = 2 * half
    link_low = precision_link[0]
    link_high = jnp.where(time_id == groups - 1, 0.0, precision_link[1])

    def flag(condition):
        return condition.astype(jnp.int32).reshape(1)

    given = swap_cores(jnp.where(row_id == 0, link_high, link_low))
    kept = jnp.where(row_id == 0, link_low, link_high)
    tops = jnp.where(row_id == 0, kept, given.T)
    bottoms = jnp.where(row_id == 0, given, kept.T)
    strip = jnp.stack([tops, bottoms])
    strip_far = swap_chips(strip)
    diag_high = packed(*gather_upper(precision_diag[1], row_id, col_id))
    w, sums_high = factor0(diag_high, size)
    diag_low = packed(*gather_upper(precision_diag[0], row_id, col_id))
    left = jnp.where(col_id == 0, strip, strip_far)
    right = jnp.where(col_id == 0, strip_far, strip)
    x = jnp.block(
        [
            [left[0], jnp.where(row_id == 0, right[0], left[1])],
            [jnp.where(row_id == 0, left[1], right[0]), right[1]],
        ]
    )
    y, gram = panel(flag(time_id >= 0), w, x)
    ahead = lax.ppermute(gram, ("tm", "row"), [(2 * t + 1, 2 * t + 3) for t in range(groups - 1)])
    near = jnp.where(row_id == 0, gram, ahead)
    link_new = link(flag(time_id % 2 == row_id), swap_cores(y), y)
    far = swap_cores(near)
    x_ahead = lax.ppermute(link_new, ("tm", "row"), [(2 * t, 2 * t + 2) for t in range(0, groups, 2)])
    x = jnp.where(row_id == 1, link_new, x_ahead)

    def own_rows(x):
        return lax.dynamic_slice_in_dim(x, col_id * half, half, 0)

    link_rows = own_rows(x)
    sums_low = jnp.ones((1, size), F32)
    for level in range(1, LEVELS):
        stride = 2 ** (level - 1)
        position = time_id // stride
        active = position % 2 == 1
        active = active & (time_id % stride == 0)
        diag_low, w, sums = factor(flag(active), diag_low, near, far, size)
        sums_low = jnp.where(active, sums, sums_low)
        y, gram = panel(flag(active), w, x)
        senders = range(stride, groups, 2 * stride)
        near = lax.ppermute(
            gram,
            ("tm", "row"),
            [(2 * t, 2 * (t - stride)) for t in senders]
            + [(2 * t + 1, 2 * (t + stride) + 1) for t in senders if t + stride < groups],
        )
        if level + 1 < LEVELS:
            odd = position // 2 % 2
            link_new = link(flag(active & (odd == row_id)), swap_cores(y), y)
            far = swap_cores(near)
            x = lax.ppermute(
                link_new,
                ("tm", "row"),
                [(2 * t, 2 * (t + stride)) for t in senders[::2]]
                + [(2 * t + 1, 2 * (t - stride) + 1) for t in senders[1::2]],
            )
            link_rows = link_rows + own_rows(x)
        else:
            link_new = link(flag(active & (row_id == 1)), swap_cores(y), y)
            far = swap_cores(near)
            link_rows = link_rows + lax.ppermute(
                own_rows(link_new), ("tm", "row"), [(2 * t + 1, 2 * (t - stride) + 1) for t in senders]
            )
    remaining = time_id % 2 ** (LEVELS - 1) == 0
    diag_low, w, sums = factor(flag(remaining), diag_low, near, far, size)
    sums_low = jnp.where(remaining, sums, sums_low)
    to_top = lax.ppermute(link_rows[:, :half], "row", [(1, 0)])
    link_low = jnp.where(row_id == 0, to_top, link_rows[:, half:]).T
    pivots = jnp.stack([own_tile(diag_low, row_id, col_id, half), precision_diag[1]])
    couplings = jnp.stack([link_low, link_high])
    sums = jnp.concatenate([sums_low, sums_high], 0)
    quarter = size // 4
    logs = jnp.log(lax.dynamic_slice_in_dim(sums, (2 * row_id + col_id) * quarter, quarter, 1))
    return (pivots, couplings, logs)


def solution(mesh):
    in_specs = (P("tm", "row", "col"), P("tm", "row", "col"))
    out_specs = (P("tm", "row", "col"), P("tm", "row", "col"), P("tm", ("row", "col")))
    return jax.shard_map(shards, mesh=mesh, in_specs=in_specs, out_specs=out_specs, check_vma=False)
```

```python
import jax
import jax.numpy as jnp
from jax import lax
from jax.experimental import pallas as pl
from jax.experimental.pallas import tpu as pltpu
from jax.sharding import PartitionSpec as P

LEVELS = 4
LEAF = 32
TILE = 128
BF16 = jnp.bfloat16
F32 = jnp.float32


def upper_blocks(count):
    return [(i, j) for i in range(count) for j in range(i, count)]


def split(x, terms):
    out = []
    for i in range(terms):
        head = x.astype(BF16)
        out.append(head)
        if i + 1 < terms:
            x = x - head.astype(F32)
    return out


PAIRS = {2: ((1, 0), (0, 1), (0, 0)), 3: ((2, 0), (0, 2), (1, 1), (1, 0), (0, 1), (0, 0))}


def dot_of(left, right, dims):
    terms = len(left)
    total = None
    for i, j in PAIRS[terms]:
        part = lax.dot_general(left[i], right[j], (dims, ((), ())), preferred_element_type=F32)
        total = part if total is None else total + part
    return total


def stacked_tn(left, right, terms):
    lefts, rights = split(left, terms), split(right, terms)
    order = PAIRS[terms]
    return lax.dot_general(
        jnp.concatenate([lefts[i] for i, _ in order], 0),
        jnp.concatenate([rights[j] for _, j in order], 0),
        (((0,), (0,)), ((), ())),
        preferred_element_type=F32,
    )


def eliminated_rows(rows, offset):
    count, width = rows.shape
    row_ids = lax.broadcasted_iota(jnp.int32, (count, width), 0)
    col_ids = lax.broadcasted_iota(jnp.int32, (count, width), 1)
    sub_ids = lax.broadcasted_iota(jnp.int32, (8, 128), 0)
    groups = count // 8
    columns = []
    for j in range(count):
        first = j // 8
        spread = jnp.broadcast_to(
            rows[8 * first :, offset + j : offset + j + 1], (count - 8 * first, 128)
        )
        columns.append([spread[8 * i : 8 * i + 8] for i in range(groups - first)])
    inside = (col_ids >= offset) & (col_ids < offset + count)
    start = jnp.where(inside, (col_ids == row_ids + offset).astype(F32), rows)
    natural = [start[8 * g : 8 * g + 8] for g in range(groups)]
    scales = [jnp.zeros((8, 128), F32) for _ in range(groups)]

    def wide(x):
        return jnp.concatenate([x] * (width // 128), 1)

    for k in range(count):
        g, s = k // 8, k % 8
        pivot = columns[k][0][s : s + 1]
        inverse = 1.0 / pivot
        scales[g] = jnp.where(sub_ids == s, lax.rsqrt(pivot), scales[g])
        factors = [c * inverse for c in columns[k]]
        factors[0] = jnp.where(sub_ids > s, factors[0], 0.0)
        for j in range(k + 1, count):
            first = j // 8
            entry = columns[k][first - g][j % 8 : j % 8 + 1]
            for i in range(groups - first):
                columns[j][i] = columns[j][i] - factors[first - g + i] * entry
        row = natural[g][s : s + 1]
        for i in range(g, groups):
            natural[i] = natural[i] - wide(factors[i - g]) * row
    return jnp.concatenate([wide(scales[g]) * natural[g] for g in range(groups)], 0)


def factor_body(w_ref):
    size = w_ref.shape[0]
    col_ids = lax.broadcasted_iota(jnp.int32, (1, size), 1)
    total = jnp.zeros((1, size), F32)
    for offset in range(0, size, LEAF):
        end = offset + LEAF
        rows = eliminated_rows(w_ref[offset:end, :], offset)
        final = jnp.where(col_ids < end, rows, 0.0)
        w_ref[offset:end, :] = final
        total = total + jnp.sum(final * final, axis=0, keepdims=True)
        if end < size:
            update = stacked_tn(rows[:, end:], rows, 3)
            old = jnp.where((col_ids >= offset) & (col_ids < end), 0.0, w_ref[end:, :])
            w_ref[end:, :] = old - update
    return total


def put_blocks(blocks_ref, w_ref):
    for b, (i, j) in enumerate(upper_blocks(w_ref.shape[0] // TILE)):
        w_ref[i * TILE : (i + 1) * TILE, j * TILE : (j + 1) * TILE] = blocks_ref[b]
        if i != j:
            w_ref[j * TILE : (j + 1) * TILE, i * TILE : (i + 1) * TILE] = jnp.zeros(
                (TILE, TILE), F32
            )


def put_tiles(ids_ref, gathered, which, w_ref):
    own, crossed, core_own, core_crossed = gathered
    half = own.shape[1]
    for row in range(2):
        for col in range(2):

            @pl.when((ids_ref[1] == row) & (ids_ref[2] == col))
            def _(row=row, col=col):
                own0, crossed0 = (own, crossed) if row == 0 else (core_own, core_crossed)
                own1, crossed1 = (core_own, core_crossed) if row == 0 else (own, crossed)
                w_ref[:half, :half] = (own0 if col == 0 else crossed0)[which]
                w_ref[:half, half:] = own1[which].T if col == 0 else own0[which]
                w_ref[half:, half:] = (crossed1 if col == 0 else own1)[which]


def clear_lower(w_ref):
    for i in range(1, w_ref.shape[0] // TILE):
        w_ref[i * TILE : (i + 1) * TILE, : i * TILE] = jnp.zeros((TILE, i * TILE), F32)


def factor_first_kernel(ids_ref, own, crossed, core_own, core_crossed, w_ref, sums_ref):
    put_tiles(ids_ref, (own, crossed, core_own, core_crossed), 1, w_ref)
    clear_lower(w_ref)
    sums_ref[...] = factor_body(w_ref)


def factor_second_kernel(
    ids_ref, own, crossed, core_own, core_crossed, near_ref, far_ref, new_ref, w_ref, sums_ref
):
    put_tiles(ids_ref, (own, crossed, core_own, core_crossed), 0, w_ref)
    for b, (i, j) in enumerate(upper_blocks(w_ref.shape[0] // TILE)):
        block = w_ref[i * TILE : (i + 1) * TILE, j * TILE : (j + 1) * TILE]
        new_ref[b] = block - near_ref[b] - far_ref[b]
    sums_ref[...] = jnp.ones_like(sums_ref)

    @pl.when(ids_ref[0] != 0)
    def _():
        put_blocks(new_ref, w_ref)
        sums_ref[...] = factor_body(w_ref)


def factor_kernel(ids_ref, diag_ref, near_ref, far_ref, before_ref, new_ref, w_ref, sums_ref):
    new_ref[...] = diag_ref[...] - near_ref[...] - far_ref[...]
    sums_ref[...] = before_ref[...]

    @pl.when(ids_ref[0] != 0)
    def _():
        put_blocks(new_ref, w_ref)
        sums_ref[...] = factor_body(w_ref)


def factor_last_kernel(
    ids_ref, diag_ref, near_ref, far_ref, before_ref, high_sums_ref, own_ref, pivots_ref, logs_ref, new_ref, w_ref, sums_ref
):
    new_ref[...] = diag_ref[...] - near_ref[...] - far_ref[...]
    sums_ref[...] = before_ref[...]
    half = own_ref.shape[1]
    per = half // TILE
    at = {ij: b for b, ij in enumerate(upper_blocks(2 * per))}
    pivots_ref[1] = own_ref[1]
    for row in range(2):
        for col in range(2):

            @pl.when((ids_ref[1] == row) & (ids_ref[2] == col))
            def _(row=row, col=col):
                for i in range(per):
                    for j in range(per):
                        a, b = row * per + i, col * per + j
                        block = new_ref[at[a, b]] if a <= b else new_ref[at[b, a]].T
                        pivots_ref[0, i * TILE : (i + 1) * TILE, j * TILE : (j + 1) * TILE] = block

    @pl.when(ids_ref[0] != 0)
    def _():
        put_blocks(new_ref, w_ref)
        sums_ref[...] = factor_body(w_ref)

    quarter = logs_ref.shape[1]
    here = pl.ds(pl.multiple_of((2 * ids_ref[1] + ids_ref[2]) * quarter, quarter), quarter)
    logs_ref[0:1, :] = jnp.log(sums_ref[:, here])
    logs_ref[1:2, :] = jnp.log(high_sums_ref[:, here])


def panel_body(w_ref, x_ref, y_ref, gram_ref):
    size = w_ref.shape[0]
    x_parts = split(x_ref[...], 3)
    for i in range(size // TILE):
        end = (i + 1) * TILE
        w_parts = split(w_ref[i * TILE : end, :end], 3)
        y_ref[i * TILE : end, :] = dot_of(w_parts, [p[:end] for p in x_parts], ((1,), (0,)))
    y_parts = split(y_ref[...], 3)
    block = 0
    for i in range(size // TILE):
        left = [p[:, i * TILE : (i + 1) * TILE] for p in y_parts]
        strip = dot_of(left, [p[:, i * TILE :] for p in y_parts], ((0,), (0,)))
        for j in range(i, size // TILE):
            gram_ref[block] = strip[:, (j - i) * TILE : (j - i + 1) * TILE]
            block += 1


def panel_first_kernel(ids_ref, w_ref, own_ref, far_ref, y_ref, gram_ref, x_ref):
    half = own_ref.shape[1]
    for row in range(2):
        for col in range(2):

            @pl.when((ids_ref[1] == row) & (ids_ref[2] == col))
            def _(row=row, col=col):
                left, right = (own_ref, far_ref) if col == 0 else (far_ref, own_ref)
                for i in range(2):
                    rows = slice(i * half, (i + 1) * half)
                    if row == 0:
                        x_ref[rows, :half] = left[i]
                        x_ref[rows, half:] = right[i]
                    else:
                        x_ref[:half, rows] = left[i].T
                        x_ref[half:, rows] = right[i].T

    panel_body(w_ref, x_ref, y_ref, gram_ref)


def panel_kernel(ids_ref, w_ref, x_ref, *refs):
    before, (y_ref, gram_ref, top_ref, bottom_ref) = refs[:-4], refs[-4:]
    half = top_ref.shape[0]

    @pl.when(ids_ref[0] != 0)
    def _():
        here = pl.ds(pl.multiple_of(ids_ref[2] * half, half), half)
        top_ref[...] = x_ref[here, :half]
        bottom_ref[...] = x_ref[here, half:]
        panel_body(w_ref, x_ref, y_ref, gram_ref)

    @pl.when(ids_ref[0] == 0)
    def _():
        for ref, old in zip((top_ref, bottom_ref), before or (None, None)):
            ref[...] = jnp.zeros_like(ref) if old is None else old[...]


def link_kernel(ids_ref, other_ref, y_ref, new_ref):
    @pl.when(ids_ref[0] != 0)
    def _():
        size = y_ref.shape[0]
        y_parts = split(y_ref[...], 3)
        other_parts = split(other_ref[...], 3)
        for i in range(size // TILE):
            left = [p[:, i * TILE : (i + 1) * TILE] for p in other_parts]
            new_ref[i * TILE : (i + 1) * TILE, :] = -dot_of(left, y_parts, ((0,), (0,)))


def link_last_kernel(ids_ref, other_ref, y_ref, new_ref):
    half = new_ref.shape[0]

    def halved(ref, which):
        return split(ref[:, pl.ds(pl.multiple_of(which * half, half), half)], 3)

    @pl.when((ids_ref[0] != 0) & (ids_ref[1] == 0))
    def _():
        new_ref[...] = -dot_of(halved(other_ref, 0), halved(y_ref, ids_ref[2]), ((0,), (0,)))

    @pl.when((ids_ref[0] != 0) & (ids_ref[1] == 1))
    def _():
        new_ref[...] = -dot_of(halved(y_ref, 1), halved(other_ref, ids_ref[2]), ((0,), (0,)))


def couplings_kernel(ids_ref, last_ref, top_ref, bottom_ref, link_ref, out_ref):
    @pl.when(ids_ref[0] != 0)
    def _():
        out_ref[0] = last_ref[...]

    @pl.when((ids_ref[0] == 0) & (ids_ref[1] == 0))
    def _():
        out_ref[0] = top_ref[...].T

    @pl.when((ids_ref[0] == 0) & (ids_ref[1] == 1))
    def _():
        out_ref[0] = bottom_ref[...].T

    out_ref[1] = jnp.where(ids_ref[3] != 0, 0.0, link_ref[1])


SMEM = pl.BlockSpec(memory_space=pltpu.SMEM)
VMEM = pl.BlockSpec(memory_space=pltpu.VMEM)


def run(kernel, ids, operands, outs, scratch=()):
    return pl.pallas_call(
        kernel,
        out_shape=tuple(jax.ShapeDtypeStruct(shape, F32) for shape in outs),
        in_specs=[SMEM] + [VMEM] * len(operands),
        out_specs=tuple(VMEM for _ in outs),
        scratch_shapes=[pltpu.VMEM(shape, F32) for shape in scratch],
        compiler_params=pltpu.CompilerParams(vmem_limit_bytes=24 * 1024 * 1024),
        cost_estimate=pl.CostEstimate(flops=1000, bytes_accessed=1000, transcendentals=0),
    )(ids, *operands)


def swap_cores(x):
    return lax.ppermute(x, "row", [(0, 1), (1, 0)])


def swap_chips(x):
    return lax.ppermute(x, "col", [(0, 1), (1, 0)])


def shards(precision_diag, precision_link):
    row_id = lax.axis_index("row")
    col_id = lax.axis_index("col")
    time_id = lax.axis_index("tm")
    groups = lax.axis_size("tm")
    half = precision_diag.shape[1]
    size = 2 * half
    full = (size, size)
    tile = (half, half)
    blocks = (len(upper_blocks(size // TILE)), TILE, TILE)
    line = (1, size)

    def ids(condition):
        return jnp.stack(
            [condition.astype(jnp.int32), row_id, col_id, (time_id == groups - 1).astype(jnp.int32)]
        )

    def tm_cores(x, pairs):
        return lax.ppermute(x, ("tm", "row"), pairs)

    crossed = lax.ppermute(precision_diag, ("row", "col"), [(0, 1), (3, 2)])
    link_got = swap_cores(precision_link)
    core_own = swap_cores(precision_diag)
    core_crossed = swap_cores(crossed)
    gathered = (precision_diag, crossed, core_own, core_crossed)
    above = jnp.where(time_id == groups - 1, 0.0, jnp.stack([link_got[1], precision_link[1]]))
    strip = jnp.where(row_id == 0, jnp.stack([precision_link[0], link_got[0]]), above)
    strip_far = swap_chips(strip)
    always = ids(time_id >= 0)
    w, sums_high = run(factor_first_kernel, always, gathered, (full, line))
    y, gram = run(panel_first_kernel, always, (w, strip, strip_far), (full, blocks), (full,))
    near = tm_cores(
        gram,
        [(2 * t + 1, 2 * t + 3) for t in range(groups - 1)] + [(2 * t, 2 * t) for t in range(groups)],
    )
    (link_new,) = run(link_kernel, ids(time_id % 2 == row_id), (swap_cores(y), y), (full,))
    x = tm_cores(
        link_new,
        [(2 * t, 2 * t + 2) for t in range(0, groups, 2)]
        + [(2 * t + 1, 2 * t + 1) for t in range(1, groups, 2)],
    )
    far = swap_cores(near)
    edges = ()
    for level in range(1, LEVELS):
        stride = 2 ** (level - 1)
        position = time_id // stride
        active = (position % 2 == 1) & (time_id % stride == 0)
        now = ids(active)
        if level == 1:
            diag_low, w, sums_low = run(
                factor_second_kernel, now, (*gathered, near, far), (blocks, full, line)
            )
        else:
            diag_low, w, sums_low = run(
                factor_kernel, now, (diag_low, near, far, sums_low), (blocks, full, line)
            )
        y, gram, *edges = run(panel_kernel, now, (w, x, *edges), (full, blocks, tile, tile))
        senders = range(stride, groups, 2 * stride)
        near = tm_cores(
            gram,
            [(2 * t, 2 * (t - stride)) for t in senders]
            + [(2 * t + 1, 2 * (t + stride) + 1) for t in senders if t + stride < groups],
        )
        other = swap_cores(y)
        if level + 1 < LEVELS:
            odd = position // 2 % 2
            (link_new,) = run(link_kernel, ids(active & (odd == row_id)), (other, y), (full,))
            x = tm_cores(
                link_new,
                [(2 * t, 2 * (t + stride)) for t in senders[::2]]
                + [(2 * t + 1, 2 * (t - stride) + 1) for t in senders[1::2]],
            )
        else:
            (link_new,) = run(link_last_kernel, now, (other, y), (tile,))
            link_last = lax.ppermute(link_new, "tm", [(t, t - stride) for t in senders])
        far = swap_cores(near)
    remaining = ids(time_id % 2 ** (LEVELS - 1) == 0)
    to_top = lax.ppermute(edges[0], "row", [(1, 0)])
    pivots, logs = run(
        factor_last_kernel,
        remaining,
        (diag_low, near, far, sums_low, sums_high, precision_diag),
        ((2, *tile), (2, size // 4)),
        (blocks, full, line),
    )
    (couplings,) = run(
        couplings_kernel, remaining, (link_last, to_top, edges[1], precision_link), ((2, *tile),)
    )
    return (pivots, couplings, logs)


def solution(mesh):
    in_specs = (P("tm", "row", "col"), P("tm", "row", "col"))
    out_specs = (P("tm", "row", "col"), P("tm", "row", "col"), P("tm", ("row", "col")))
    return jax.shard_map(shards, mesh=mesh, in_specs=in_specs, out_specs=out_specs, check_vma=False)
```

```python
import jax
import jax.numpy as jnp
from jax import lax
from jax.experimental import pallas as pl
from jax.experimental.pallas import tpu as pltpu
from jax.sharding import PartitionSpec as P

LEVELS = 4
LEAF = 32
STEP = 16
TILE = 128
BF16 = jnp.bfloat16
F32 = jnp.float32


def upper_blocks(count):
    return [(i, j) for i in range(count) for j in range(i, count)]


def split(x, terms):
    out = []
    for i in range(terms):
        head = x.astype(BF16)
        out.append(head)
        if i + 1 < terms:
            x = x - head.astype(F32)
    return out


PAIRS = {2: ((1, 0), (0, 1), (0, 0)), 3: ((2, 0), (0, 2), (1, 1), (1, 0), (0, 1), (0, 0))}


def dot_of(left, right, dims):
    terms = len(left)
    total = None
    for i, j in PAIRS[terms]:
        part = lax.dot_general(left[i], right[j], (dims, ((), ())), preferred_element_type=F32)
        total = part if total is None else total + part
    return total


def stacked(x, side):
    parts = split(x, 3)
    return jnp.concatenate([parts[pair[side]] for pair in PAIRS[3]], 0)


def product_tn(left, right):
    return lax.dot_general(left, right, (((0,), (0,)), ((), ())), preferred_element_type=F32)


def eliminated_rows(rows, offset):
    count, width = rows.shape
    groups = count // 8
    sub_ids = lax.broadcasted_iota(jnp.int32, (8, 128), 0)
    row_ids = lax.broadcasted_iota(jnp.int32, (8, width), 0)
    col_ids = lax.broadcasted_iota(jnp.int32, (8, width), 1)
    natural = [rows[8 * g : 8 * g + 8] for g in range(groups)]
    scales = [jnp.zeros((8, 128), F32) for _ in range(groups)]

    def wide(x):
        return jnp.concatenate([x] * (width // 128), 1)

    for start in range(0, count, STEP):
        columns = {}
        for j in range(start, start + STEP):
            at = offset + j
            columns[j] = {
                i: jnp.broadcast_to(natural[i][:, at : at + 1], (8, 128))
                for i in range(j // 8, groups)
            }
        inside = (col_ids >= offset + start) & (col_ids < offset + start + STEP)
        for i in range(groups):
            one = start <= 8 * i < start + STEP
            put = (col_ids == row_ids + (offset + 8 * i)).astype(F32) if one else 0.0
            natural[i] = jnp.where(inside, put, natural[i])
        for k in range(start, start + STEP):
            g, s = k // 8, k % 8
            pivot = columns[k][g][s : s + 1]
            inverse = 1.0 / pivot
            scales[g] = jnp.where(sub_ids == s, lax.rsqrt(pivot), scales[g])
            factors = {i: columns[k][i] * inverse for i in range(g, groups)}
            factors[g] = jnp.where(sub_ids > s, factors[g], 0.0)
            for j in range(k + 1, start + STEP):
                entry = columns[k][j // 8][j % 8 : j % 8 + 1]
                for i in range(j // 8, groups):
                    columns[j][i] = columns[j][i] - factors[i] * entry
            row = natural[g][s : s + 1]
            for i in range(g, groups):
                natural[i] = natural[i] - wide(factors[i]) * row
    return jnp.concatenate([wide(scales[g]) * natural[g] for g in range(groups)], 0)


def factor_body(w_ref):
    size = w_ref.shape[0]
    col_ids = lax.broadcasted_iota(jnp.int32, (1, size), 1)
    total = jnp.zeros((1, size), F32)
    for low in range(0, size, TILE):
        high = low + TILE
        done = []
        left = w_ref[low:high, :]
        for offset in range(low, high, LEAF):
            end = offset + LEAF
            rows = eliminated_rows(left[:LEAF], offset)
            if end < high:
                old = jnp.where((col_ids >= offset) & (col_ids < end), 0.0, left[LEAF:])
                left = old - product_tn(stacked(rows[:, end:high], 0), stacked(rows, 1))
            rows = jnp.where((col_ids >= end) & (col_ids < high), 0.0, rows)
            done.append(rows)
            final = jnp.where(col_ids < high, rows, 0.0)
            w_ref[offset:end, :] = final
            total = total + jnp.sum(final * final, axis=0, keepdims=True)
        if high == size:
            break
        panel_rows = jnp.concatenate(done, 0)
        lefts, rights = stacked(panel_rows[:, high:], 0), stacked(panel_rows, 1)
        for first in range(high, size, TILE):
            strip = slice(first, first + TILE)
            part = lefts[:, first - high : first - high + TILE]
            old = jnp.where(col_ids[:, :high] >= low, 0.0, w_ref[strip, :high])
            w_ref[strip, :high] = old - product_tn(part, rights[:, :high])
            w_ref[strip, first:] = w_ref[strip, first:] - product_tn(part, rights[:, first:])
    return total


def put_blocks(blocks_ref, w_ref):
    for b, (i, j) in enumerate(upper_blocks(w_ref.shape[0] // TILE)):
        w_ref[i * TILE : (i + 1) * TILE, j * TILE : (j + 1) * TILE] = blocks_ref[b]
        if i != j:
            w_ref[j * TILE : (j + 1) * TILE, i * TILE : (i + 1) * TILE] = jnp.zeros(
                (TILE, TILE), F32
            )


def put_tiles(ids_ref, gathered, which, w_ref):
    own, crossed, core_own, core_crossed = gathered
    half = own.shape[1]
    for row in range(2):
        for col in range(2):

            @pl.when((ids_ref[1] == row) & (ids_ref[2] == col))
            def _(row=row, col=col):
                own0, crossed0 = (own, crossed) if row == 0 else (core_own, core_crossed)
                own1, crossed1 = (core_own, core_crossed) if row == 0 else (own, crossed)
                w_ref[:half, :half] = (own0 if col == 0 else crossed0)[which]
                w_ref[:half, half:] = own1[which].T if col == 0 else own0[which]
                w_ref[half:, half:] = (crossed1 if col == 0 else own1)[which]


def clear_lower(w_ref):
    for i in range(1, w_ref.shape[0] // TILE):
        w_ref[i * TILE : (i + 1) * TILE, : i * TILE] = jnp.zeros((TILE, i * TILE), F32)


def factor_first_kernel(ids_ref, own, crossed, core_own, core_crossed, w_ref, sums_ref):
    put_tiles(ids_ref, (own, crossed, core_own, core_crossed), 1, w_ref)
    clear_lower(w_ref)
    sums_ref[...] = factor_body(w_ref)


def factor_second_kernel(
    ids_ref, own, crossed, core_own, core_crossed, near_ref, far_ref, new_ref, w_ref, sums_ref
):
    put_tiles(ids_ref, (own, crossed, core_own, core_crossed), 0, w_ref)
    for b, (i, j) in enumerate(upper_blocks(w_ref.shape[0] // TILE)):
        block = w_ref[i * TILE : (i + 1) * TILE, j * TILE : (j + 1) * TILE]
        new_ref[b] = block - near_ref[b] - far_ref[b]
    sums_ref[...] = jnp.ones_like(sums_ref)

    @pl.when(ids_ref[0] != 0)
    def _():
        put_blocks(new_ref, w_ref)
        sums_ref[...] = factor_body(w_ref)


def factor_kernel(ids_ref, diag_ref, near_ref, far_ref, before_ref, new_ref, w_ref, sums_ref):
    new_ref[...] = diag_ref[...] - near_ref[...] - far_ref[...]
    sums_ref[...] = before_ref[...]

    @pl.when(ids_ref[0] != 0)
    def _():
        put_blocks(new_ref, w_ref)
        sums_ref[...] = factor_body(w_ref)


def factor_last_kernel(
    ids_ref, diag_ref, near_ref, far_ref, before_ref, high_sums_ref, own_ref, pivots_ref, logs_ref, new_ref, w_ref, sums_ref
):
    new_ref[...] = diag_ref[...] - near_ref[...] - far_ref[...]
    sums_ref[...] = before_ref[...]
    half = own_ref.shape[1]
    per = half // TILE
    at = {ij: b for b, ij in enumerate(upper_blocks(2 * per))}
    pivots_ref[1] = own_ref[1]
    for row in range(2):
        for col in range(2):

            @pl.when((ids_ref[1] == row) & (ids_ref[2] == col))
            def _(row=row, col=col):
                for i in range(per):
                    for j in range(per):
                        a, b = row * per + i, col * per + j
                        block = new_ref[at[a, b]] if a <= b else new_ref[at[b, a]].T
                        pivots_ref[0, i * TILE : (i + 1) * TILE, j * TILE : (j + 1) * TILE] = block

    @pl.when(ids_ref[0] != 0)
    def _():
        put_blocks(new_ref, w_ref)
        sums_ref[...] = factor_body(w_ref)

    quarter = logs_ref.shape[1]
    here = pl.ds(pl.multiple_of((2 * ids_ref[1] + ids_ref[2]) * quarter, quarter), quarter)
    logs_ref[0:1, :] = jnp.log(sums_ref[:, here])
    logs_ref[1:2, :] = jnp.log(high_sums_ref[:, here])


def panel_body(w_ref, x_ref, y_ref, gram_ref):
    size = w_ref.shape[0]
    x_parts = split(x_ref[...], 3)
    for i in range(size // TILE):
        end = (i + 1) * TILE
        w_parts = split(w_ref[i * TILE : end, :end], 3)
        y_ref[i * TILE : end, :] = dot_of(w_parts, [p[:end] for p in x_parts], ((1,), (0,)))
    y_parts = split(y_ref[...], 3)
    block = 0
    for i in range(size // TILE):
        left = [p[:, i * TILE : (i + 1) * TILE] for p in y_parts]
        strip = dot_of(left, [p[:, i * TILE :] for p in y_parts], ((0,), (0,)))
        for j in range(i, size // TILE):
            gram_ref[block] = strip[:, (j - i) * TILE : (j - i + 1) * TILE]
            block += 1


def strip_kernel(ids_ref, link_ref, got_ref, strip_ref):
    @pl.when(ids_ref[1] == 0)
    def _():
        strip_ref[0] = link_ref[0]
        strip_ref[1] = got_ref[0]

    @pl.when(ids_ref[1] != 0)
    def _():
        live = ids_ref[3] == 0
        strip_ref[0] = jnp.where(live, got_ref[1], 0.0).T
        strip_ref[1] = jnp.where(live, link_ref[1], 0.0).T


def panel_first_kernel(ids_ref, w_ref, own_ref, far_ref, y_ref, gram_ref, x_ref):
    half = own_ref.shape[1]
    below, first = ids_ref[1] == 0, ids_ref[2] == 0
    left = [jnp.where(first, own_ref[i], far_ref[i]) for i in range(2)]
    right = [jnp.where(first, far_ref[i], own_ref[i]) for i in range(2)]
    x_ref[:half, :half] = left[0]
    x_ref[half:, half:] = right[1]
    x_ref[:half, half:] = jnp.where(below, right[0], left[1])
    x_ref[half:, :half] = jnp.where(below, left[1], right[0])
    panel_body(w_ref, x_ref, y_ref, gram_ref)


def panel_kernel(ids_ref, w_ref, x_ref, *refs):
    before, (y_ref, gram_ref, top_ref, bottom_ref) = refs[:-4], refs[-4:]
    half = top_ref.shape[0]

    @pl.when(ids_ref[0] != 0)
    def _():
        here = pl.ds(pl.multiple_of(ids_ref[2] * half, half), half)
        top_ref[...] = x_ref[here, :half]
        bottom_ref[...] = x_ref[here, half:]
        panel_body(w_ref, x_ref, y_ref, gram_ref)

    @pl.when(ids_ref[0] == 0)
    def _():
        for ref, old in zip((top_ref, bottom_ref), before or (None, None)):
            ref[...] = jnp.zeros_like(ref) if old is None else old[...]


def link_kernel(ids_ref, other_ref, y_ref, new_ref):
    @pl.when(ids_ref[0] != 0)
    def _():
        size = y_ref.shape[0]
        y_parts = split(y_ref[...], 3)
        other_parts = split(other_ref[...], 3)
        for i in range(size // TILE):
            left = [p[:, i * TILE : (i + 1) * TILE] for p in other_parts]
            new_ref[i * TILE : (i + 1) * TILE, :] = -dot_of(left, y_parts, ((0,), (0,)))


def link_last_kernel(ids_ref, other_ref, y_ref, new_ref):
    half = new_ref.shape[0]

    def halved(ref, which):
        return split(ref[:, pl.ds(pl.multiple_of(which * half, half), half)], 3)

    @pl.when((ids_ref[0] != 0) & (ids_ref[1] == 0))
    def _():
        new_ref[...] = -dot_of(halved(other_ref, 0), halved(y_ref, ids_ref[2]), ((0,), (0,)))

    @pl.when((ids_ref[0] != 0) & (ids_ref[1] == 1))
    def _():
        new_ref[...] = -dot_of(halved(y_ref, 1), halved(other_ref, ids_ref[2]), ((0,), (0,)))


def couplings_kernel(ids_ref, last_ref, top_ref, bottom_ref, link_ref, out_ref):
    @pl.when(ids_ref[0] != 0)
    def _():
        out_ref[0] = last_ref[...]

    @pl.when((ids_ref[0] == 0) & (ids_ref[1] == 0))
    def _():
        out_ref[0] = top_ref[...].T

    @pl.when((ids_ref[0] == 0) & (ids_ref[1] == 1))
    def _():
        out_ref[0] = bottom_ref[...].T

    out_ref[1] = jnp.where(ids_ref[3] != 0, 0.0, link_ref[1])


SMEM = pl.BlockSpec(memory_space=pltpu.SMEM)
VMEM = pl.BlockSpec(memory_space=pltpu.VMEM)


def run(kernel, ids, operands, outs, scratch=(), after=(), flops=1000):
    count = 1 + len(operands)

    def body(*refs):
        kernel(*refs[:count], *refs[count + len(after) :])

    return pl.pallas_call(
        body,
        out_shape=tuple(jax.ShapeDtypeStruct(shape, F32) for shape in outs),
        in_specs=[SMEM] + [VMEM] * len(operands) + [pl.BlockSpec(memory_space=pl.ANY)] * len(after),
        out_specs=tuple(VMEM for _ in outs),
        scratch_shapes=[pltpu.VMEM(shape, F32) for shape in scratch],
        compiler_params=pltpu.CompilerParams(vmem_limit_bytes=24 * 1024 * 1024),
        cost_estimate=pl.CostEstimate(flops=flops, bytes_accessed=1000, transcendentals=0),
    )(ids, *operands, *after)


def swap_cores(x):
    return lax.ppermute(x, "row", [(0, 1), (1, 0)])


def swap_chips(x):
    return lax.ppermute(x, "col", [(0, 1), (1, 0)])


def shards(precision_diag, precision_link):
    row_id = lax.axis_index("row")
    col_id = lax.axis_index("col")
    time_id = lax.axis_index("tm")
    groups = lax.axis_size("tm")
    half = precision_diag.shape[1]
    size = 2 * half
    full = (size, size)
    tile = (half, half)
    blocks = (len(upper_blocks(size // TILE)), TILE, TILE)
    line = (1, size)

    def ids(condition):
        return jnp.stack(
            [condition.astype(jnp.int32), row_id, col_id, (time_id == groups - 1).astype(jnp.int32)]
        )

    def tm_cores(x, pairs):
        return lax.ppermute(x, ("tm", "row"), pairs)

    crossed = lax.ppermute(precision_diag, ("row", "col"), [(0, 1), (3, 2)])
    link_got = swap_cores(precision_link)
    core_own = swap_cores(precision_diag)
    core_crossed = swap_cores(crossed)
    gathered = (precision_diag, crossed, core_own, core_crossed)
    always = ids(time_id >= 0)
    (strip,) = run(strip_kernel, always, (precision_link, link_got), ((2, *tile),))
    strip_far = swap_chips(strip)
    w, sums_high = run(factor_first_kernel, always, gathered, (full, line))
    y, gram = run(panel_first_kernel, always, (w, strip, strip_far), (full, blocks), (full,))
    near = tm_cores(
        gram,
        [(2 * t + 1, 2 * t + 3) for t in range(groups - 1)] + [(2 * t, 2 * t) for t in range(groups)],
    )
    other = swap_cores(y)
    far = swap_cores(near)
    (link_new,) = run(link_kernel, ids(time_id % 2 == row_id), (other, y), (full,), after=(far,))
    x = tm_cores(
        link_new,
        [(2 * t, 2 * t + 2) for t in range(0, groups, 2)]
        + [(2 * t + 1, 2 * t + 1) for t in range(1, groups, 2)],
    )
    edges = ()
    for level in range(1, LEVELS):
        stride = 2 ** (level - 1)
        position = time_id // stride
        active = (position % 2 == 1) & (time_id % stride == 0)
        now = ids(active)
        if level == 1:
            diag_low, w, sums_low = run(
                factor_second_kernel, now, (*gathered, near, far), (blocks, full, line), flops=2000000000
            )
        else:
            diag_low, w, sums_low = run(
                factor_kernel, now, (diag_low, near, far, sums_low), (blocks, full, line), flops=2000000000
            )
        y, gram, *edges = run(panel_kernel, now, (w, x, *edges), (full, blocks, tile, tile))
        senders = range(stride, groups, 2 * stride)
        near = tm_cores(
            gram,
            [(2 * t, 2 * (t - stride)) for t in senders]
            + [(2 * t + 1, 2 * (t + stride) + 1) for t in senders if t + stride < groups],
        )
        other = swap_cores(y)
        far = swap_cores(near)
        if level + 1 < LEVELS:
            odd = position // 2 % 2
            (link_new,) = run(
                link_kernel, ids(active & (odd == row_id)), (other, y), (full,), after=(far,)
            )
            x = tm_cores(
                link_new,
                [(2 * t, 2 * (t + stride)) for t in senders[::2]]
                + [(2 * t + 1, 2 * (t - stride) + 1) for t in senders[1::2]],
            )
        else:
            (link_new,) = run(link_last_kernel, now, (other, y), (tile,))
            link_last = lax.ppermute(link_new, "tm", [(t, t - stride) for t in senders])
    remaining = ids(time_id % 2 ** (LEVELS - 1) == 0)
    to_top = lax.ppermute(edges[0], "row", [(1, 0)])
    pivots, logs = run(
        factor_last_kernel,
        remaining,
        (diag_low, near, far, sums_low, sums_high, precision_diag),
        ((2, *tile), (2, size // 4)),
        (blocks, full, line),
    )
    (couplings,) = run(
        couplings_kernel, remaining, (link_last, to_top, edges[1], precision_link), ((2, *tile),), after=(logs,)
    )
    return (pivots, couplings, logs)


def solution(mesh):
    in_specs = (P("tm", "row", "col"), P("tm", "row", "col"))
    out_specs = (P("tm", "row", "col"), P("tm", "row", "col"), P("tm", ("row", "col")))
    return jax.shard_map(shards, mesh=mesh, in_specs=in_specs, out_specs=out_specs, check_vma=False)
```

```python
import jax
import jax.numpy as jnp
from jax import lax
from jax.experimental import pallas as pl
from jax.experimental.pallas import tpu as pltpu
from jax.sharding import PartitionSpec as P

LEVELS = 4
LEAF = 32
STEP = 16
TILE = 128
BF16 = jnp.bfloat16
F32 = jnp.float32


def upper_blocks(count):
    return [(i, j) for i in range(count) for j in range(i, count)]


def split(x, terms):
    out = []
    for i in range(terms):
        head = x.astype(BF16)
        out.append(head)
        if i + 1 < terms:
            x = x - head.astype(F32)
    return out


PAIRS = {2: ((1, 0), (0, 1), (0, 0)), 3: ((2, 0), (0, 2), (1, 1), (1, 0), (0, 1), (0, 0))}


def dot_of(left, right, dims):
    terms = len(left)
    total = None
    for i, j in PAIRS[terms]:
        part = lax.dot_general(left[i], right[j], (dims, ((), ())), preferred_element_type=F32)
        total = part if total is None else total + part
    return total


def stacked(x, side):
    parts = split(x, 3)
    return jnp.concatenate([parts[pair[side]] for pair in PAIRS[3]], 0)


def product_tn(left, right):
    return lax.dot_general(left, right, (((0,), (0,)), ((), ())), preferred_element_type=F32)


def eliminated_rows(rows, offset):
    count, width = rows.shape
    groups = count // 8
    sub_ids = lax.broadcasted_iota(jnp.int32, (8, 128), 0)
    row_ids = lax.broadcasted_iota(jnp.int32, (8, width), 0)
    col_ids = lax.broadcasted_iota(jnp.int32, (8, width), 1)
    natural = [rows[8 * g : 8 * g + 8] for g in range(groups)]
    scales = [jnp.zeros((8, 128), F32) for _ in range(groups)]

    def wide(x):
        return jnp.concatenate([x] * (width // 128), 1)

    for start in range(0, count, STEP):
        columns = {}
        for j in range(start, start + STEP):
            at = offset + j
            columns[j] = {
                i: jnp.broadcast_to(natural[i][:, at : at + 1], (8, 128))
                for i in range(j // 8, groups)
            }
        inside = (col_ids >= offset + start) & (col_ids < offset + start + STEP)
        for i in range(groups):
            one = start <= 8 * i < start + STEP
            put = (col_ids == row_ids + (offset + 8 * i)).astype(F32) if one else 0.0
            natural[i] = jnp.where(inside, put, natural[i])
        for k in range(start, start + STEP):
            g, s = k // 8, k % 8
            pivot = columns[k][g][s : s + 1]
            inverse = 1.0 / pivot
            scales[g] = jnp.where(sub_ids == s, lax.rsqrt(pivot), scales[g])
            factors = {i: columns[k][i] * inverse for i in range(g, groups)}
            factors[g] = jnp.where(sub_ids > s, factors[g], 0.0)
            for j in range(k + 1, start + STEP):
                entry = columns[k][j // 8][j % 8 : j % 8 + 1]
                for i in range(j // 8, groups):
                    columns[j][i] = columns[j][i] - factors[i] * entry
            row = natural[g][s : s + 1]
            for i in range(g, groups):
                natural[i] = natural[i] - wide(factors[i]) * row
    return jnp.concatenate([wide(scales[g]) * natural[g] for g in range(groups)], 0)


def factor_body(w_ref):
    size = w_ref.shape[0]
    col_ids = lax.broadcasted_iota(jnp.int32, (1, size), 1)
    total = jnp.zeros((1, size), F32)
    for low in range(0, size, TILE):
        high = low + TILE
        done = []
        left = w_ref[low:high, :]
        for offset in range(low, high, LEAF):
            end = offset + LEAF
            rows = eliminated_rows(left[:LEAF], offset)
            if end < high:
                old = jnp.where((col_ids >= offset) & (col_ids < end), 0.0, left[LEAF:])
                left = old - product_tn(stacked(rows[:, end:high], 0), stacked(rows, 1))
            rows = jnp.where((col_ids >= end) & (col_ids < high), 0.0, rows)
            done.append(rows)
            final = jnp.where(col_ids < high, rows, 0.0)
            w_ref[offset:end, :] = final
            total = total + jnp.sum(final * final, axis=0, keepdims=True)
        if high == size:
            break
        panel_rows = jnp.concatenate(done, 0)
        lefts, rights = stacked(panel_rows[:, high:], 0), stacked(panel_rows, 1)
        for first in range(high, size, TILE):
            strip = slice(first, first + TILE)
            part = lefts[:, first - high : first - high + TILE]
            old = jnp.where(col_ids[:, :high] >= low, 0.0, w_ref[strip, :high])
            w_ref[strip, :high] = old - product_tn(part, rights[:, :high])
            w_ref[strip, first:] = w_ref[strip, first:] - product_tn(part, rights[:, first:])
    return total


def put_blocks(blocks_ref, w_ref):
    for b, (i, j) in enumerate(upper_blocks(w_ref.shape[0] // TILE)):
        w_ref[i * TILE : (i + 1) * TILE, j * TILE : (j + 1) * TILE] = blocks_ref[b]
        if i != j:
            w_ref[j * TILE : (j + 1) * TILE, i * TILE : (i + 1) * TILE] = jnp.zeros(
                (TILE, TILE), F32
            )


def put_tiles(ids_ref, gathered, which, w_ref):
    own, crossed, core_own, core_crossed = gathered
    half = own.shape[1]
    for row in range(2):
        for col in range(2):

            @pl.when((ids_ref[1] == row) & (ids_ref[2] == col))
            def _(row=row, col=col):
                own0, crossed0 = (own, crossed) if row == 0 else (core_own, core_crossed)
                own1, crossed1 = (core_own, core_crossed) if row == 0 else (own, crossed)
                w_ref[:half, :half] = (own0 if col == 0 else crossed0)[which]
                w_ref[:half, half:] = own1[which].T if col == 0 else own0[which]
                w_ref[half:, half:] = (crossed1 if col == 0 else own1)[which]


def clear_lower(w_ref):
    for i in range(1, w_ref.shape[0] // TILE):
        w_ref[i * TILE : (i + 1) * TILE, : i * TILE] = jnp.zeros((TILE, i * TILE), F32)


def factor_first_kernel(
    ids_ref, own, crossed, core_own, core_crossed, w_ref, sums_ref, low_ref
):
    gathered = (own, crossed, core_own, core_crossed)
    put_tiles(ids_ref, gathered, 0, w_ref)
    for b, (i, j) in enumerate(upper_blocks(w_ref.shape[0] // TILE)):
        low_ref[b] = w_ref[i * TILE : (i + 1) * TILE, j * TILE : (j + 1) * TILE]
    put_tiles(ids_ref, gathered, 1, w_ref)
    clear_lower(w_ref)
    sums_ref[...] = factor_body(w_ref)


def factor_kernel(ids_ref, diag_ref, near_ref, far_ref, before_ref, new_ref, w_ref, sums_ref):
    new_ref[...] = diag_ref[...] - near_ref[...] - far_ref[...]
    sums_ref[...] = before_ref[...]

    @pl.when(ids_ref[0] != 0)
    def _():
        put_blocks(new_ref, w_ref)
        sums_ref[...] = factor_body(w_ref)


def factor_last_kernel(
    ids_ref,
    diag_ref,
    near_ref,
    far_ref,
    late_ref,
    late_far_ref,
    before_ref,
    high_sums_ref,
    own_ref,
    pivots_ref,
    logs_ref,
    new_ref,
    w_ref,
    sums_ref,
):
    early = diag_ref[...] - late_ref[...] - late_far_ref[...]
    new_ref[...] = early - near_ref[...] - far_ref[...]
    sums_ref[...] = before_ref[...]
    half = own_ref.shape[1]
    per = half // TILE
    at = {ij: b for b, ij in enumerate(upper_blocks(2 * per))}
    pivots_ref[1] = own_ref[1]
    for row in range(2):
        for col in range(2):

            @pl.when((ids_ref[1] == row) & (ids_ref[2] == col))
            def _(row=row, col=col):
                for i in range(per):
                    for j in range(per):
                        a, b = row * per + i, col * per + j
                        block = new_ref[at[a, b]] if a <= b else new_ref[at[b, a]].T
                        pivots_ref[0, i * TILE : (i + 1) * TILE, j * TILE : (j + 1) * TILE] = block

    @pl.when(ids_ref[0] != 0)
    def _():
        put_blocks(new_ref, w_ref)
        sums_ref[...] = factor_body(w_ref)

    quarter = logs_ref.shape[1]
    here = pl.ds(pl.multiple_of((2 * ids_ref[1] + ids_ref[2]) * quarter, quarter), quarter)
    logs_ref[0:1, :] = jnp.log(sums_ref[:, here])
    logs_ref[1:2, :] = jnp.log(high_sums_ref[:, here])


def panel_body(w_ref, x_ref, y_ref, gram_ref):
    size = w_ref.shape[0]
    x_parts = split(x_ref[...], 3)
    for i in range(size // TILE):
        end = (i + 1) * TILE
        w_parts = split(w_ref[i * TILE : end, :end], 3)
        y_ref[i * TILE : end, :] = dot_of(w_parts, [p[:end] for p in x_parts], ((1,), (0,)))
    y_parts = split(y_ref[...], 3)
    block = 0
    for i in range(size // TILE):
        left = [p[:, i * TILE : (i + 1) * TILE] for p in y_parts]
        strip = dot_of(left, [p[:, i * TILE :] for p in y_parts], ((0,), (0,)))
        for j in range(i, size // TILE):
            gram_ref[block] = strip[:, (j - i) * TILE : (j - i + 1) * TILE]
            block += 1


def strip_kernel(ids_ref, link_ref, got_ref, strip_ref):
    @pl.when(ids_ref[1] == 0)
    def _():
        strip_ref[0] = link_ref[0]
        strip_ref[1] = got_ref[0]

    @pl.when(ids_ref[1] != 0)
    def _():
        live = ids_ref[3] == 0
        strip_ref[0] = jnp.where(live, got_ref[1], 0.0).T
        strip_ref[1] = jnp.where(live, link_ref[1], 0.0).T


def panel_first_kernel(ids_ref, w_ref, own_ref, far_ref, y_ref, gram_ref, x_ref):
    half = own_ref.shape[1]
    below, first = ids_ref[1] == 0, ids_ref[2] == 0
    left = [jnp.where(first, own_ref[i], far_ref[i]) for i in range(2)]
    right = [jnp.where(first, far_ref[i], own_ref[i]) for i in range(2)]
    x_ref[:half, :half] = left[0]
    x_ref[half:, half:] = right[1]
    x_ref[:half, half:] = jnp.where(below, right[0], left[1])
    x_ref[half:, :half] = jnp.where(below, left[1], right[0])
    panel_body(w_ref, x_ref, y_ref, gram_ref)


def panel_kernel(ids_ref, w_ref, x_ref, *refs):
    before, (y_ref, gram_ref, top_ref, bottom_ref) = refs[:-4], refs[-4:]
    half = top_ref.shape[0]

    @pl.when(ids_ref[0] != 0)
    def _():
        here = pl.ds(pl.multiple_of(ids_ref[2] * half, half), half)
        top_ref[...] = x_ref[here, :half]
        bottom_ref[...] = x_ref[here, half:]
        panel_body(w_ref, x_ref, y_ref, gram_ref)

    @pl.when(ids_ref[0] == 0)
    def _():
        for ref, old in zip((top_ref, bottom_ref), before or (None, None)):
            ref[...] = jnp.zeros_like(ref) if old is None else old[...]


def link_kernel(ids_ref, other_ref, y_ref, new_ref):
    @pl.when(ids_ref[0] != 0)
    def _():
        size = y_ref.shape[0]
        y_parts = split(y_ref[...], 3)
        other_parts = split(other_ref[...], 3)
        for i in range(size // TILE):
            left = [p[:, i * TILE : (i + 1) * TILE] for p in other_parts]
            new_ref[i * TILE : (i + 1) * TILE, :] = -dot_of(left, y_parts, ((0,), (0,)))


def link_last_kernel(ids_ref, other_ref, y_ref, new_ref):
    half = new_ref.shape[0]

    def halved(ref, which):
        return split(ref[:, pl.ds(pl.multiple_of(which * half, half), half)], 3)

    @pl.when((ids_ref[0] != 0) & (ids_ref[1] == 0))
    def _():
        new_ref[...] = -dot_of(halved(other_ref, 0), halved(y_ref, ids_ref[2]), ((0,), (0,)))

    @pl.when((ids_ref[0] != 0) & (ids_ref[1] == 1))
    def _():
        new_ref[...] = -dot_of(halved(y_ref, 1), halved(other_ref, ids_ref[2]), ((0,), (0,)))


def couplings_kernel(ids_ref, last_ref, top_ref, bottom_ref, link_ref, out_ref):
    @pl.when(ids_ref[0] != 0)
    def _():
        out_ref[0] = last_ref[...]

    @pl.when((ids_ref[0] == 0) & (ids_ref[1] == 0))
    def _():
        out_ref[0] = top_ref[...].T

    @pl.when((ids_ref[0] == 0) & (ids_ref[1] == 1))
    def _():
        out_ref[0] = bottom_ref[...].T

    out_ref[1] = jnp.where(ids_ref[3] != 0, 0.0, link_ref[1])


SMEM = pl.BlockSpec(memory_space=pltpu.SMEM)
VMEM = pl.BlockSpec(memory_space=pltpu.VMEM)
ANY = pl.BlockSpec(memory_space=pl.ANY)


def run(kernel, ids, operands, outs, scratch=(), after=(), through=(), flops=1000):
    count = 1 + len(operands)
    end = count + len(after) + len(through)

    def body(*refs):
        kernel(*refs[:count], *refs[end : end + len(outs)], *refs[end + len(outs) + len(through) :])

    return pl.pallas_call(
        body,
        out_shape=tuple(
            jax.ShapeDtypeStruct(shape, F32) for shape in (*outs, *(x.shape for x in through))
        ),
        in_specs=[SMEM] + [VMEM] * len(operands) + [ANY] * len(after + through),
        out_specs=(VMEM,) * len(outs) + (ANY,) * len(through),
        input_output_aliases={
            count + len(after) + i: len(outs) + i for i in range(len(through))
        },
        scratch_shapes=[pltpu.VMEM(shape, F32) for shape in scratch],
        compiler_params=pltpu.CompilerParams(vmem_limit_bytes=24 * 1024 * 1024),
        cost_estimate=pl.CostEstimate(flops=flops, bytes_accessed=1000, transcendentals=0),
    )(ids, *operands, *after, *through)


def swap_cores(x):
    return lax.ppermute(x, "row", [(0, 1), (1, 0)])


def swap_chips(x):
    return lax.ppermute(x, "col", [(0, 1), (1, 0)])


def shards(precision_diag, precision_link):
    row_id = lax.axis_index("row")
    col_id = lax.axis_index("col")
    time_id = lax.axis_index("tm")
    groups = lax.axis_size("tm")
    half = precision_diag.shape[1]
    size = 2 * half
    full = (size, size)
    tile = (half, half)
    blocks = (len(upper_blocks(size // TILE)), TILE, TILE)
    line = (1, size)

    def ids(condition):
        return jnp.stack(
            [condition.astype(jnp.int32), row_id, col_id, (time_id == groups - 1).astype(jnp.int32)]
        )

    def tm_cores(x, pairs):
        full_pairs = []
        for source, target in pairs:
            turned = (source < groups) != (target < groups)
            full_pairs += [(2 * source + c, 2 * target + (1 - c if turned else c)) for c in range(2)]
        return lax.ppermute(x, ("tm", "row", "col"), full_pairs)

    crossed = lax.ppermute(precision_diag, ("row", "col"), [(0, 1), (3, 2)])
    link_got = swap_cores(precision_link)
    core_own = swap_cores(precision_diag)
    core_crossed = swap_cores(crossed)
    gathered = (precision_diag, crossed, core_own, core_crossed)
    always = ids(time_id >= 0)
    (strip,) = run(strip_kernel, always, (precision_link, link_got), ((2, *tile),))
    strip_far = swap_chips(strip)
    w, sums_high, diag_low = run(factor_first_kernel, always, gathered, (full, line, blocks))
    sums_low = jnp.ones(line, F32)
    y, gram = run(panel_first_kernel, always, (w, strip, strip_far), (full, blocks), (full,))
    near = tm_cores(
        gram,
        [(2 * t + 1, 2 * t + 3) for t in range(groups - 1)] + [(2 * t, 2 * t) for t in range(groups)],
    )
    other = swap_cores(y)
    far = swap_cores(near)
    (link_new,) = run(link_kernel, ids(time_id % 2 == row_id), (other, y), (full,))
    x = tm_cores(
        link_new,
        [(2 * t, 2 * t + 2) for t in range(0, groups, 2)]
        + [(2 * t + 1, 2 * t + 1) for t in range(1, groups, 2)],
    )
    edges = ()
    for level in range(1, LEVELS):
        stride = 2 ** (level - 1)
        position = time_id // stride
        active = (position % 2 == 1) & (time_id % stride == 0)
        now = ids(active)
        diag_low, w, sums_low = run(
            factor_kernel,
            now,
            (diag_low, near, far, sums_low),
            (blocks, full, line),
            flops=2 * 10**9,
        )
        y, gram, *edges = run(panel_kernel, now, (w, x, *edges), (full, blocks, tile, tile))
        senders = range(stride, groups, 2 * stride)
        back = [(2 * t, 2 * (t - stride)) for t in senders]
        ahead = [(2 * t + 1, 2 * (t + stride) + 1) for t in senders if t + stride < groups]
        if level == 2:
            near = tm_cores(gram, ahead[::2] + back[1::2])
        else:
            near = tm_cores(gram, back + ahead)
        other = swap_cores(y)
        far = swap_cores(near)
        if level + 1 < LEVELS:
            odd = position // 2 % 2
            link_new, *rest = run(
                link_kernel,
                ids(active & (odd == row_id)),
                (other, y),
                (full,),
                after=(far,),
                through=(gram,) if level == 2 else (),
            )
            x = tm_cores(
                link_new,
                [(2 * t, 2 * (t + stride)) for t in senders[::2]]
                + [(2 * t + 1, 2 * (t - stride) + 1) for t in senders[1::2]],
            )
            if rest:
                late = tm_cores(rest[0], back[::2] + ahead[1::2])
                late_far = swap_cores(late)
        else:
            (link_new,) = run(link_last_kernel, now, (other, y), (tile,))
            link_last = lax.ppermute(link_new, "tm", [(t, t - stride) for t in senders])
    remaining = ids(time_id % 2 ** (LEVELS - 1) == 0)
    to_top = lax.ppermute(edges[0], "row", [(1, 0)])
    pivots, logs = run(
        factor_last_kernel,
        remaining,
        (diag_low, near, far, late, late_far, sums_low, sums_high, precision_diag),
        ((2, *tile), (2, size // 4)),
        (blocks, full, line),
    )
    (couplings,) = run(
        couplings_kernel, remaining, (link_last, to_top, edges[1], precision_link), ((2, *tile),), after=(logs,)
    )
    return (pivots, couplings, logs)


def solution(mesh):
    in_specs = (P("tm", "row", "col"), P("tm", "row", "col"))
    out_specs = (P("tm", "row", "col"), P("tm", "row", "col"), P("tm", ("row", "col")))
    return jax.shard_map(shards, mesh=mesh, in_specs=in_specs, out_specs=out_specs, check_vma=False)
```

```python
import jax
import jax.numpy as jnp
from jax import lax
from jax.experimental import pallas as pl
from jax.experimental.pallas import tpu as pltpu
from jax.sharding import PartitionSpec as P

LEVELS = 4
LEAF = 32
STEP = 16
TILE = 128
BF16 = jnp.bfloat16
F32 = jnp.float32


def upper_blocks(count):
    return [(i, j) for i in range(count) for j in range(i, count)]


def split(x, terms):
    out = []
    for i in range(terms):
        head = x.astype(BF16)
        out.append(head)
        if i + 1 < terms:
            x = x - head.astype(F32)
    return out


PAIRS = {2: ((1, 0), (0, 1), (0, 0)), 3: ((2, 0), (0, 2), (1, 1), (1, 0), (0, 1), (0, 0))}


def dot_of(left, right, dims):
    terms = len(left)
    total = None
    for i, j in PAIRS[terms]:
        part = lax.dot_general(left[i], right[j], (dims, ((), ())), preferred_element_type=F32)
        total = part if total is None else total + part
    return total


def stacked(x, side):
    parts = split(x, 3)
    return jnp.concatenate([parts[pair[side]] for pair in PAIRS[3]], 0)


def product_tn(left, right):
    return lax.dot_general(left, right, (((0,), (0,)), ((), ())), preferred_element_type=F32)


def eliminated_rows(rows, offset):
    count, width = rows.shape
    groups = count // 8
    sub_ids = lax.broadcasted_iota(jnp.int32, (8, 128), 0)
    row_ids = lax.broadcasted_iota(jnp.int32, (8, width), 0)
    col_ids = lax.broadcasted_iota(jnp.int32, (8, width), 1)
    natural = [rows[8 * g : 8 * g + 8] for g in range(groups)]
    scales = [jnp.zeros((8, 128), F32) for _ in range(groups)]

    def wide(x):
        return jnp.concatenate([x] * (width // 128), 1)

    for start in range(0, count, STEP):
        columns = {}
        for j in range(start, start + STEP):
            at = offset + j
            columns[j] = {
                i: jnp.broadcast_to(natural[i][:, at : at + 1], (8, 128))
                for i in range(j // 8, groups)
            }
        inside = (col_ids >= offset + start) & (col_ids < offset + start + STEP)
        for i in range(groups):
            one = start <= 8 * i < start + STEP
            put = (col_ids == row_ids + (offset + 8 * i)).astype(F32) if one else 0.0
            natural[i] = jnp.where(inside, put, natural[i])
        for k in range(start, start + STEP):
            g, s = k // 8, k % 8
            pivot = columns[k][g][s : s + 1]
            inverse = 1.0 / pivot
            scales[g] = jnp.where(sub_ids == s, lax.rsqrt(pivot), scales[g])
            factors = {i: columns[k][i] * inverse for i in range(g, groups)}
            factors[g] = jnp.where(sub_ids > s, factors[g], 0.0)
            for j in range(k + 1, start + STEP):
                entry = columns[k][j // 8][j % 8 : j % 8 + 1]
                for i in range(j // 8, groups):
                    columns[j][i] = columns[j][i] - factors[i] * entry
            row = natural[g][s : s + 1]
            for i in range(g, groups):
                natural[i] = natural[i] - wide(factors[i]) * row
    return jnp.concatenate([wide(scales[g]) * natural[g] for g in range(groups)], 0)


def factor_body(w_ref):
    size = w_ref.shape[0]
    col_ids = lax.broadcasted_iota(jnp.int32, (1, size), 1)
    total = jnp.zeros((1, size), F32)
    for low in range(0, size, TILE):
        high = low + TILE
        done = []
        left = w_ref[low:high, :]
        for offset in range(low, high, LEAF):
            end = offset + LEAF
            rows = eliminated_rows(left[:LEAF], offset)
            if end < high:
                old = jnp.where((col_ids >= offset) & (col_ids < end), 0.0, left[LEAF:])
                left = old - product_tn(stacked(rows[:, end:high], 0), stacked(rows, 1))
            rows = jnp.where((col_ids >= end) & (col_ids < high), 0.0, rows)
            done.append(rows)
            final = jnp.where(col_ids < high, rows, 0.0)
            w_ref[offset:end, :] = final
            total = total + jnp.sum(final * final, axis=0, keepdims=True)
        if high == size:
            break
        panel_rows = jnp.concatenate(done, 0)
        lefts, rights = stacked(panel_rows[:, high:], 0), stacked(panel_rows, 1)
        for first in range(high, size, TILE):
            strip = slice(first, first + TILE)
            part = lefts[:, first - high : first - high + TILE]
            old = jnp.where(col_ids[:, :high] >= low, 0.0, w_ref[strip, :high])
            w_ref[strip, :high] = old - product_tn(part, rights[:, :high])
            w_ref[strip, first:] = w_ref[strip, first:] - product_tn(part, rights[:, first:])
    return total


def fetch(copies):
    for copy in copies:
        copy.start()
    for copy in copies:
        copy.wait()


def put_blocks(blocks_ref, w_ref):
    for b, (i, j) in enumerate(upper_blocks(w_ref.shape[0] // TILE)):
        w_ref[i * TILE : (i + 1) * TILE, j * TILE : (j + 1) * TILE] = blocks_ref[b]
        if i != j:
            w_ref[j * TILE : (j + 1) * TILE, i * TILE : (i + 1) * TILE] = jnp.zeros(
                (TILE, TILE), F32
            )


def put_tiles(ids_ref, gathered, which, w_ref):
    own, crossed, core_own, core_crossed = gathered
    half = own.shape[1]
    for row in range(2):
        for col in range(2):

            @pl.when((ids_ref[1] == row) & (ids_ref[2] == col))
            def _(row=row, col=col):
                own0, crossed0 = (own, crossed) if row == 0 else (core_own, core_crossed)
                own1, crossed1 = (core_own, core_crossed) if row == 0 else (own, crossed)
                w_ref[:half, :half] = (own0 if col == 0 else crossed0)[which]
                w_ref[:half, half:] = own1[which].T if col == 0 else own0[which]
                w_ref[half:, half:] = (crossed1 if col == 0 else own1)[which]


def clear_lower(w_ref):
    for i in range(1, w_ref.shape[0] // TILE):
        w_ref[i * TILE : (i + 1) * TILE, : i * TILE] = jnp.zeros((TILE, i * TILE), F32)


def factor_first_kernel(
    ids_ref, own, crossed, core_own, core_crossed, w_ref, sums_ref, low_ref
):
    gathered = (own, crossed, core_own, core_crossed)
    put_tiles(ids_ref, gathered, 0, w_ref)
    for b, (i, j) in enumerate(upper_blocks(w_ref.shape[0] // TILE)):
        low_ref[b] = w_ref[i * TILE : (i + 1) * TILE, j * TILE : (j + 1) * TILE]
    put_tiles(ids_ref, gathered, 1, w_ref)
    clear_lower(w_ref)
    sums_ref[...] = factor_body(w_ref)


def factor_kernel(copies, ids_ref, diag_ref, near_ref, far_ref, before_ref, new_ref, w_ref, sums_ref):
    fetch(copies)
    new_ref[...] = diag_ref[...] - near_ref[...] - far_ref[...]
    sums_ref[...] = before_ref[...]

    @pl.when(ids_ref[0] != 0)
    def _():
        put_blocks(new_ref, w_ref)
        sums_ref[...] = factor_body(w_ref)


def factor_last_kernel(
    copies,
    ids_ref,
    diag_ref,
    near_ref,
    far_ref,
    before_ref,
    high_sums_ref,
    own_ref,
    pivots_ref,
    logs_ref,
    new_ref,
    w_ref,
    sums_ref,
):
    fetch(copies)
    new_ref[...] = diag_ref[...] - near_ref[...] - far_ref[...]
    sums_ref[...] = before_ref[...]
    half = own_ref.shape[1]
    per = half // TILE
    at = {ij: b for b, ij in enumerate(upper_blocks(2 * per))}
    pivots_ref[1] = own_ref[1]
    for row in range(2):
        for col in range(2):

            @pl.when((ids_ref[1] == row) & (ids_ref[2] == col))
            def _(row=row, col=col):
                for i in range(per):
                    for j in range(per):
                        a, b = row * per + i, col * per + j
                        block = new_ref[at[a, b]] if a <= b else new_ref[at[b, a]].T
                        pivots_ref[0, i * TILE : (i + 1) * TILE, j * TILE : (j + 1) * TILE] = block

    @pl.when(ids_ref[0] != 0)
    def _():
        put_blocks(new_ref, w_ref)
        sums_ref[...] = factor_body(w_ref)

    quarter = logs_ref.shape[1]
    here = pl.ds(pl.multiple_of((2 * ids_ref[1] + ids_ref[2]) * quarter, quarter), quarter)
    logs_ref[0:1, :] = jnp.log(sums_ref[:, here])
    logs_ref[1:2, :] = jnp.log(high_sums_ref[:, here])


def panel_body(w_ref, x_ref, y_ref, gram_ref):
    size = w_ref.shape[0]
    x_parts = split(x_ref[...], 3)
    for i in range(size // TILE):
        end = (i + 1) * TILE
        w_parts = split(w_ref[i * TILE : end, :end], 3)
        y_ref[i * TILE : end, :] = dot_of(w_parts, [p[:end] for p in x_parts], ((1,), (0,)))
    y_parts = split(y_ref[...], 3)
    block = 0
    for i in range(size // TILE):
        left = [p[:, i * TILE : (i + 1) * TILE] for p in y_parts]
        strip = dot_of(left, [p[:, i * TILE :] for p in y_parts], ((0,), (0,)))
        for j in range(i, size // TILE):
            gram_ref[block] = strip[:, (j - i) * TILE : (j - i + 1) * TILE]
            block += 1


def strip_kernel(ids_ref, link_ref, got_ref, strip_ref):
    @pl.when(ids_ref[1] == 0)
    def _():
        strip_ref[0] = link_ref[0]
        strip_ref[1] = got_ref[0]

    @pl.when(ids_ref[1] != 0)
    def _():
        live = ids_ref[3] == 0
        strip_ref[0] = jnp.where(live, got_ref[1], 0.0).T
        strip_ref[1] = jnp.where(live, link_ref[1], 0.0).T


def panel_first_kernel(ids_ref, w_ref, own_ref, far_ref, y_ref, gram_ref, x_ref):
    half = own_ref.shape[1]
    below, first = ids_ref[1] == 0, ids_ref[2] == 0
    left = [jnp.where(first, own_ref[i], far_ref[i]) for i in range(2)]
    right = [jnp.where(first, far_ref[i], own_ref[i]) for i in range(2)]
    x_ref[:half, :half] = left[0]
    x_ref[half:, half:] = right[1]
    x_ref[:half, half:] = jnp.where(below, right[0], left[1])
    x_ref[half:, :half] = jnp.where(below, left[1], right[0])
    panel_body(w_ref, x_ref, y_ref, gram_ref)


def panel_kernel(ids_ref, w_ref, x_ref, *refs):
    before, (y_ref, gram_ref, top_ref, bottom_ref) = refs[:-4], refs[-4:]
    half = top_ref.shape[0]

    @pl.when(ids_ref[0] != 0)
    def _():
        here = pl.ds(pl.multiple_of(ids_ref[2] * half, half), half)
        top_ref[...] = x_ref[here, :half]
        bottom_ref[...] = x_ref[here, half:]
        panel_body(w_ref, x_ref, y_ref, gram_ref)

    @pl.when(ids_ref[0] == 0)
    def _():
        for ref, old in zip((top_ref, bottom_ref), before or (None, None)):
            ref[...] = jnp.zeros_like(ref) if old is None else old[...]


def link_kernel(copies, ids_ref, other_ref, y_ref, new_ref):
    @pl.when(ids_ref[0] != 0)
    def _():
        fetch(copies)
        size = y_ref.shape[0]
        y_parts = split(y_ref[...], 3)
        other_parts = split(other_ref[...], 3)
        for i in range(size // TILE):
            left = [p[:, i * TILE : (i + 1) * TILE] for p in other_parts]
            new_ref[i * TILE : (i + 1) * TILE, :] = -dot_of(left, y_parts, ((0,), (0,)))


def link_last_kernel(copies, ids_ref, other_ref, y_ref, new_ref):
    half = new_ref.shape[0]

    def halved(ref, which):
        return split(ref[:, pl.ds(pl.multiple_of(which * half, half), half)], 3)

    @pl.when((ids_ref[0] != 0) & (ids_ref[1] == 0))
    def _():
        fetch(copies)
        new_ref[...] = -dot_of(halved(other_ref, 0), halved(y_ref, ids_ref[2]), ((0,), (0,)))

    @pl.when((ids_ref[0] != 0) & (ids_ref[1] == 1))
    def _():
        fetch(copies)
        new_ref[...] = -dot_of(halved(y_ref, 1), halved(other_ref, ids_ref[2]), ((0,), (0,)))


def couplings_kernel(ids_ref, last_ref, top_ref, bottom_ref, link_ref, out_ref):
    @pl.when(ids_ref[0] != 0)
    def _():
        out_ref[0] = last_ref[...]

    @pl.when((ids_ref[0] == 0) & (ids_ref[1] == 0))
    def _():
        out_ref[0] = top_ref[...].T

    @pl.when((ids_ref[0] == 0) & (ids_ref[1] == 1))
    def _():
        out_ref[0] = bottom_ref[...].T

    out_ref[1] = jnp.where(ids_ref[3] != 0, 0.0, link_ref[1])


SMEM = pl.BlockSpec(memory_space=pltpu.SMEM)
VMEM = pl.BlockSpec(memory_space=pltpu.VMEM)
ANY = pl.BlockSpec(memory_space=pl.ANY)


def run(kernel, ids, operands, outs, scratch=(), after=(), lazy=0, flops=1000):
    count = 1 + len(operands)
    end = count + len(after)
    tail = end + len(outs) + len(scratch)

    def body(*refs):
        if not lazy:
            return kernel(*refs[:count], *refs[end:])
        places, sems = refs[tail : tail + lazy], refs[tail + lazy]
        copies = [
            pltpu.make_async_copy(refs[1 + i], places[i], sems.at[i]) for i in range(lazy)
        ]
        kernel(copies, refs[0], *places, *refs[1 + lazy : count], *refs[end:tail])

    scratch_shapes = [pltpu.VMEM(shape, F32) for shape in scratch]
    if lazy:
        scratch_shapes += [pltpu.VMEM(x.shape, F32) for x in operands[:lazy]]
        scratch_shapes += [pltpu.SemaphoreType.DMA((lazy,))]
    return pl.pallas_call(
        body,
        out_shape=tuple(jax.ShapeDtypeStruct(shape, F32) for shape in outs),
        in_specs=[SMEM] + [ANY] * lazy + [VMEM] * (len(operands) - lazy) + [ANY] * len(after),
        out_specs=tuple(VMEM for _ in outs),
        scratch_shapes=scratch_shapes,
        compiler_params=pltpu.CompilerParams(vmem_limit_bytes=24 * 1024 * 1024),
        cost_estimate=pl.CostEstimate(flops=flops, bytes_accessed=1000, transcendentals=0),
    )(ids, *operands, *after)


def swap_cores(x):
    return lax.ppermute(x, "row", [(0, 1), (1, 0)])


def swap_chips(x):
    return lax.ppermute(x, "col", [(0, 1), (1, 0)])


def shards(precision_diag, precision_link):
    row_id = lax.axis_index("row")
    col_id = lax.axis_index("col")
    time_id = lax.axis_index("tm")
    groups = lax.axis_size("tm")
    half = precision_diag.shape[1]
    size = 2 * half
    full = (size, size)
    tile = (half, half)
    blocks = (len(upper_blocks(size // TILE)), TILE, TILE)
    line = (1, size)

    def ids(condition):
        return jnp.stack(
            [condition.astype(jnp.int32), row_id, col_id, (time_id == groups - 1).astype(jnp.int32)]
        )

    def tm_cores(x, pairs):
        return lax.ppermute(x, ("tm", "row"), pairs)

    crossed = lax.ppermute(precision_diag, ("row", "col"), [(0, 1), (3, 2)])
    link_got = swap_cores(precision_link)
    core_own = swap_cores(precision_diag)
    core_crossed = swap_cores(crossed)
    gathered = (precision_diag, crossed, core_own, core_crossed)
    always = ids(time_id >= 0)
    (strip,) = run(strip_kernel, always, (precision_link, link_got), ((2, *tile),))
    strip_far = swap_chips(strip)
    w, sums_high, diag_low = run(factor_first_kernel, always, gathered, (full, line, blocks))
    sums_low = jnp.ones(line, F32)
    y, gram = run(panel_first_kernel, always, (w, strip, strip_far), (full, blocks), (full,))
    near = tm_cores(
        gram,
        [(2 * t + 1, 2 * t + 3) for t in range(groups - 1)] + [(2 * t, 2 * t) for t in range(groups)],
    )
    other = swap_cores(y)
    far = swap_cores(near)
    (link_new,) = run(link_kernel, ids(time_id % 2 == row_id), (other, y), (full,), lazy=2)
    x = tm_cores(
        link_new,
        [(2 * t, 2 * t + 2) for t in range(0, groups, 2)]
        + [(2 * t + 1, 2 * t + 1) for t in range(1, groups, 2)],
    )
    edges = ()
    for level in range(1, LEVELS):
        stride = 2 ** (level - 1)
        position = time_id // stride
        active = (position % 2 == 1) & (time_id % stride == 0)
        now = ids(active)
        diag_low, w, sums_low = run(
            factor_kernel,
            now,
            (diag_low, near, far, sums_low),
            (blocks, full, line),
            lazy=3,
            flops=2 * 10**9,
        )
        y, gram, *edges = run(panel_kernel, now, (w, x, *edges), (full, blocks, tile, tile))
        senders = range(stride, groups, 2 * stride)
        back = [(2 * t, 2 * (t - stride)) for t in senders]
        ahead = [(2 * t + 1, 2 * (t + stride) + 1) for t in senders if t + stride < groups]
        near = tm_cores(gram, back + ahead)
        other = swap_cores(y)
        far = swap_cores(near)
        if level + 1 < LEVELS:
            odd = position // 2 % 2
            (link_new,) = run(
                link_kernel, ids(active & (odd == row_id)), (other, y), (full,), after=(far,), lazy=2
            )
            x = tm_cores(
                link_new,
                [(2 * t, 2 * (t + stride)) for t in senders[::2]]
                + [(2 * t + 1, 2 * (t - stride) + 1) for t in senders[1::2]],
            )
        else:
            (link_new,) = run(link_last_kernel, now, (other, y), (tile,), lazy=2)
            link_last = lax.ppermute(link_new, "tm", [(t, t - stride) for t in senders])
    remaining = ids(time_id % 2 ** (LEVELS - 1) == 0)
    to_top = lax.ppermute(edges[0], "row", [(1, 0)])
    pivots, logs = run(
        factor_last_kernel,
        remaining,
        (diag_low, near, far, sums_low, sums_high, precision_diag),
        ((2, *tile), (2, size // 4)),
        (blocks, full, line),
        lazy=3,
    )
    (couplings,) = run(
        couplings_kernel, remaining, (link_last, to_top, edges[1], precision_link), ((2, *tile),), after=(logs,)
    )
    return (pivots, couplings, logs)


def solution(mesh):
    in_specs = (P("tm", "row", "col"), P("tm", "row", "col"))
    out_specs = (P("tm", "row", "col"), P("tm", "row", "col"), P("tm", ("row", "col")))
    return jax.shard_map(shards, mesh=mesh, in_specs=in_specs, out_specs=out_specs, check_vma=False)
```

```python
import jax
import jax.numpy as jnp
from jax import lax
from jax.experimental import pallas as pl
from jax.experimental.pallas import tpu as pltpu
from jax.sharding import PartitionSpec as P

LEVELS = 4
LEAF = 32
STEP = 16
TILE = 128
BF16 = jnp.bfloat16
F32 = jnp.float32


def upper_blocks(count):
    return [(i, j) for i in range(count) for j in range(i, count)]


def split(x, terms):
    out = []
    for i in range(terms):
        head = x.astype(BF16)
        out.append(head)
        if i + 1 < terms:
            x = x - head.astype(F32)
    return out


PAIRS = {2: ((1, 0), (0, 1), (0, 0)), 3: ((2, 0), (0, 2), (1, 1), (1, 0), (0, 1), (0, 0))}


def dot_of(left, right, dims):
    terms = len(left)
    total = None
    for i, j in PAIRS[terms]:
        part = lax.dot_general(left[i], right[j], (dims, ((), ())), preferred_element_type=F32)
        total = part if total is None else total + part
    return total


def stacked(x, side):
    parts = split(x, 3)
    return jnp.concatenate([parts[pair[side]] for pair in PAIRS[3]], 0)


def product_tn(left, right):
    return lax.dot_general(left, right, (((0,), (0,)), ((), ())), preferred_element_type=F32)


def eliminated_rows(rows, offset):
    count, width = rows.shape
    groups = count // 8
    sub_ids = lax.broadcasted_iota(jnp.int32, (8, 128), 0)
    row_ids = lax.broadcasted_iota(jnp.int32, (8, width), 0)
    col_ids = lax.broadcasted_iota(jnp.int32, (8, width), 1)
    natural = [rows[8 * g : 8 * g + 8] for g in range(groups)]
    scales = [jnp.zeros((8, 128), F32) for _ in range(groups)]

    def wide(x):
        return jnp.concatenate([x] * (width // 128), 1)

    for start in range(0, count, STEP):
        columns = {}
        for j in range(start, start + STEP):
            at = offset + j
            columns[j] = {
                i: jnp.broadcast_to(natural[i][:, at : at + 1], (8, 128))
                for i in range(j // 8, groups)
            }
        inside = (col_ids >= offset + start) & (col_ids < offset + start + STEP)
        for i in range(groups):
            one = start <= 8 * i < start + STEP
            put = (col_ids == row_ids + (offset + 8 * i)).astype(F32) if one else 0.0
            natural[i] = jnp.where(inside, put, natural[i])
        for k in range(start, start + STEP):
            g, s = k // 8, k % 8
            pivot = columns[k][g][s : s + 1]
            inverse = 1.0 / pivot
            scales[g] = jnp.where(sub_ids == s, lax.rsqrt(pivot), scales[g])
            factors = {i: columns[k][i] * inverse for i in range(g, groups)}
            factors[g] = jnp.where(sub_ids > s, factors[g], 0.0)
            for j in range(k + 1, start + STEP):
                entry = columns[k][j // 8][j % 8 : j % 8 + 1]
                for i in range(j // 8, groups):
                    columns[j][i] = columns[j][i] - factors[i] * entry
            row = natural[g][s : s + 1]
            for i in range(g, groups):
                natural[i] = natural[i] - wide(factors[i]) * row
    return jnp.concatenate([wide(scales[g]) * natural[g] for g in range(groups)], 0)


def factor_body(w_ref):
    size = w_ref.shape[0]
    col_ids = lax.broadcasted_iota(jnp.int32, (1, size), 1)
    total = jnp.zeros((1, size), F32)
    for low in range(0, size, TILE):
        high = low + TILE
        done = []
        left = w_ref[low:high, :]
        for offset in range(low, high, LEAF):
            end = offset + LEAF
            rows = eliminated_rows(left[:LEAF], offset)
            if end < high:
                old = jnp.where((col_ids >= offset) & (col_ids < end), 0.0, left[LEAF:])
                left = old - product_tn(stacked(rows[:, end:high], 0), stacked(rows, 1))
            rows = jnp.where((col_ids >= end) & (col_ids < high), 0.0, rows)
            done.append(rows)
            final = jnp.where(col_ids < high, rows, 0.0)
            w_ref[offset:end, :] = final
            total = total + jnp.sum(final * final, axis=0, keepdims=True)
        if high == size:
            break
        panel_rows = jnp.concatenate(done, 0)
        lefts, rights = stacked(panel_rows[:, high:], 0), stacked(panel_rows, 1)
        for first in range(high, size, TILE):
            strip = slice(first, first + TILE)
            part = lefts[:, first - high : first - high + TILE]
            old = jnp.where(col_ids[:, :high] >= low, 0.0, w_ref[strip, :high])
            w_ref[strip, :high] = old - product_tn(part, rights[:, :high])
            w_ref[strip, first:] = w_ref[strip, first:] - product_tn(part, rights[:, first:])
    return total


def fetch(copies):
    for copy in copies:
        copy.start()
    for copy in copies:
        copy.wait()


def put_blocks(blocks_ref, w_ref):
    for b, (i, j) in enumerate(upper_blocks(w_ref.shape[0] // TILE)):
        w_ref[i * TILE : (i + 1) * TILE, j * TILE : (j + 1) * TILE] = blocks_ref[b]
        if i != j:
            w_ref[j * TILE : (j + 1) * TILE, i * TILE : (i + 1) * TILE] = jnp.zeros(
                (TILE, TILE), F32
            )


def put_tiles(ids_ref, gathered, which, w_ref):
    own, crossed, core_own, core_crossed = gathered
    half = own.shape[1]
    for row in range(2):
        for col in range(2):

            @pl.when((ids_ref[1] == row) & (ids_ref[2] == col))
            def _(row=row, col=col):
                own0, crossed0 = (own, crossed) if row == 0 else (core_own, core_crossed)
                own1, crossed1 = (core_own, core_crossed) if row == 0 else (own, crossed)
                w_ref[:half, :half] = (own0 if col == 0 else crossed0)[which]
                w_ref[:half, half:] = own1[which].T if col == 0 else own0[which]
                w_ref[half:, half:] = (crossed1 if col == 0 else own1)[which]


def clear_lower(w_ref):
    for i in range(1, w_ref.shape[0] // TILE):
        w_ref[i * TILE : (i + 1) * TILE, : i * TILE] = jnp.zeros((TILE, i * TILE), F32)


def factor_first_kernel(
    ids_ref, own, crossed, core_own, core_crossed, w_ref, sums_ref, low_ref
):
    gathered = (own, crossed, core_own, core_crossed)
    put_tiles(ids_ref, gathered, 0, w_ref)
    for b, (i, j) in enumerate(upper_blocks(w_ref.shape[0] // TILE)):
        low_ref[b] = w_ref[i * TILE : (i + 1) * TILE, j * TILE : (j + 1) * TILE]
    put_tiles(ids_ref, gathered, 1, w_ref)
    clear_lower(w_ref)
    sums_ref[...] = factor_body(w_ref)


def factor_kernel(copies, ids_ref, diag_ref, near_ref, far_ref, before_ref, new_ref, w_ref, sums_ref):
    fetch(copies)
    new_ref[...] = diag_ref[...] - near_ref[...] - far_ref[...]
    sums_ref[...] = before_ref[...]

    @pl.when(ids_ref[0] != 0)
    def _():
        put_blocks(new_ref, w_ref)
        sums_ref[...] = factor_body(w_ref)


def factor_last_kernel(
    copies,
    ids_ref,
    diag_ref,
    near_ref,
    far_ref,
    before_ref,
    high_sums_ref,
    own_ref,
    pivots_ref,
    logs_ref,
    new_ref,
    w_ref,
    sums_ref,
):
    fetch(copies)
    new_ref[...] = diag_ref[...] - near_ref[...] - far_ref[...]
    sums_ref[...] = before_ref[...]
    half = own_ref.shape[1]
    per = half // TILE
    at = {ij: b for b, ij in enumerate(upper_blocks(2 * per))}
    pivots_ref[1] = own_ref[1]
    for row in range(2):
        for col in range(2):

            @pl.when((ids_ref[1] == row) & (ids_ref[2] == col))
            def _(row=row, col=col):
                for i in range(per):
                    for j in range(per):
                        a, b = row * per + i, col * per + j
                        block = new_ref[at[a, b]] if a <= b else new_ref[at[b, a]].T
                        pivots_ref[0, i * TILE : (i + 1) * TILE, j * TILE : (j + 1) * TILE] = block

    @pl.when(ids_ref[0] != 0)
    def _():
        put_blocks(new_ref, w_ref)
        sums_ref[...] = factor_body(w_ref)

    quarter = logs_ref.shape[1]
    here = pl.ds(pl.multiple_of((2 * ids_ref[1] + ids_ref[2]) * quarter, quarter), quarter)
    logs_ref[0:1, :] = jnp.log(sums_ref[:, here])
    logs_ref[1:2, :] = jnp.log(high_sums_ref[:, here])


def panel_body(w_ref, x_ref, y_ref, gram_ref):
    size = w_ref.shape[0]
    x_parts = split(x_ref[...], 3)
    for i in range(size // TILE):
        end = (i + 1) * TILE
        w_parts = split(w_ref[i * TILE : end, :end], 3)
        y_ref[i * TILE : end, :] = dot_of(w_parts, [p[:end] for p in x_parts], ((1,), (0,)))
    y_parts = split(y_ref[...], 3)
    block = 0
    for i in range(size // TILE):
        left = [p[:, i * TILE : (i + 1) * TILE] for p in y_parts]
        strip = dot_of(left, [p[:, i * TILE :] for p in y_parts], ((0,), (0,)))
        for j in range(i, size // TILE):
            gram_ref[block] = strip[:, (j - i) * TILE : (j - i + 1) * TILE]
            block += 1


def strip_kernel(ids_ref, link_ref, got_ref, strip_ref):
    @pl.when(ids_ref[1] == 0)
    def _():
        strip_ref[0] = link_ref[0]
        strip_ref[1] = got_ref[0]

    @pl.when(ids_ref[1] != 0)
    def _():
        live = ids_ref[3] == 0
        strip_ref[0] = jnp.where(live, got_ref[1], 0.0).T
        strip_ref[1] = jnp.where(live, link_ref[1], 0.0).T


def panel_first_kernel(ids_ref, w_ref, own_ref, far_ref, y_ref, gram_ref, x_ref):
    half = own_ref.shape[1]
    below, first = ids_ref[1] == 0, ids_ref[2] == 0
    left = [jnp.where(first, own_ref[i], far_ref[i]) for i in range(2)]
    right = [jnp.where(first, far_ref[i], own_ref[i]) for i in range(2)]
    x_ref[:half, :half] = left[0]
    x_ref[half:, half:] = right[1]
    x_ref[:half, half:] = jnp.where(below, right[0], left[1])
    x_ref[half:, :half] = jnp.where(below, left[1], right[0])
    panel_body(w_ref, x_ref, y_ref, gram_ref)


def panel_kernel(ids_ref, w_ref, x_ref, *refs):
    before, (y_ref, gram_ref, top_ref, bottom_ref) = refs[:-4], refs[-4:]
    half = top_ref.shape[0]

    @pl.when(ids_ref[0] != 0)
    def _():
        here = pl.ds(pl.multiple_of(ids_ref[2] * half, half), half)
        top_ref[...] = x_ref[here, :half]
        bottom_ref[...] = x_ref[here, half:]
        panel_body(w_ref, x_ref, y_ref, gram_ref)

    @pl.when(ids_ref[0] == 0)
    def _():
        for ref, old in zip((top_ref, bottom_ref), before or (None, None)):
            ref[...] = jnp.zeros_like(ref) if old is None else old[...]


def link_kernel(copies, ids_ref, other_ref, y_ref, out_ref, new_ref):
    @pl.when(ids_ref[0] != 0)
    def _():
        fetch(copies)
        size = y_ref.shape[0]
        y_parts = split(y_ref[...], 3)
        other_parts = split(other_ref[...], 3)
        for i in range(size // TILE):
            left = [p[:, i * TILE : (i + 1) * TILE] for p in other_parts]
            new_ref[i * TILE : (i + 1) * TILE, :] = -dot_of(left, y_parts, ((0,), (0,)))
        pltpu.sync_copy(new_ref, out_ref)


def link_last_kernel(copies, ids_ref, other_ref, y_ref, new_ref):
    half = new_ref.shape[0]

    def halved(ref, which):
        return split(ref[:, pl.ds(pl.multiple_of(which * half, half), half)], 3)

    @pl.when((ids_ref[0] != 0) & (ids_ref[1] == 0))
    def _():
        fetch(copies)
        new_ref[...] = -dot_of(halved(other_ref, 0), halved(y_ref, ids_ref[2]), ((0,), (0,)))

    @pl.when((ids_ref[0] != 0) & (ids_ref[1] == 1))
    def _():
        fetch(copies)
        new_ref[...] = -dot_of(halved(y_ref, 1), halved(other_ref, ids_ref[2]), ((0,), (0,)))


def couplings_kernel(ids_ref, last_ref, top_ref, bottom_ref, link_ref, out_ref):
    @pl.when(ids_ref[0] != 0)
    def _():
        out_ref[0] = last_ref[...]

    @pl.when((ids_ref[0] == 0) & (ids_ref[1] == 0))
    def _():
        out_ref[0] = top_ref[...].T

    @pl.when((ids_ref[0] == 0) & (ids_ref[1] == 1))
    def _():
        out_ref[0] = bottom_ref[...].T

    out_ref[1] = jnp.where(ids_ref[3] != 0, 0.0, link_ref[1])


SMEM = pl.BlockSpec(memory_space=pltpu.SMEM)
VMEM = pl.BlockSpec(memory_space=pltpu.VMEM)
ANY = pl.BlockSpec(memory_space=pl.ANY)


def run(kernel, ids, operands, outs, scratch=(), after=(), lazy=0, flops=1000, out=VMEM):
    count = 1 + len(operands)
    end = count + len(after)
    tail = end + len(outs) + len(scratch)

    def body(*refs):
        if not lazy:
            return kernel(*refs[:count], *refs[end:])
        places, sems = refs[tail : tail + lazy], refs[tail + lazy]
        copies = [
            pltpu.make_async_copy(refs[1 + i], places[i], sems.at[i]) for i in range(lazy)
        ]
        kernel(copies, refs[0], *places, *refs[1 + lazy : count], *refs[end:tail])

    scratch_shapes = [pltpu.VMEM(shape, F32) for shape in scratch]
    if lazy:
        scratch_shapes += [pltpu.VMEM(x.shape, F32) for x in operands[:lazy]]
        scratch_shapes += [pltpu.SemaphoreType.DMA((lazy,))]
    return pl.pallas_call(
        body,
        out_shape=tuple(jax.ShapeDtypeStruct(shape, F32) for shape in outs),
        in_specs=[SMEM] + [ANY] * lazy + [VMEM] * (len(operands) - lazy) + [ANY] * len(after),
        out_specs=tuple(out for _ in outs),
        scratch_shapes=scratch_shapes,
        compiler_params=pltpu.CompilerParams(vmem_limit_bytes=24 * 1024 * 1024),
        cost_estimate=pl.CostEstimate(flops=flops, bytes_accessed=1000, transcendentals=0),
    )(ids, *operands, *after)


def swap_cores(x):
    return lax.ppermute(x, "row", [(0, 1), (1, 0)])


def swap_chips(x):
    return lax.ppermute(x, "col", [(0, 1), (1, 0)])


def shards(precision_diag, precision_link):
    row_id = lax.axis_index("row")
    col_id = lax.axis_index("col")
    time_id = lax.axis_index("tm")
    groups = lax.axis_size("tm")
    half = precision_diag.shape[1]
    size = 2 * half
    full = (size, size)
    tile = (half, half)
    blocks = (len(upper_blocks(size // TILE)), TILE, TILE)
    line = (1, size)

    def ids(condition):
        return jnp.stack(
            [condition.astype(jnp.int32), row_id, col_id, (time_id == groups - 1).astype(jnp.int32)]
        )

    def tm_cores(x, pairs):
        return lax.ppermute(x, ("tm", "row"), pairs)

    crossed = lax.ppermute(precision_diag, ("row", "col"), [(0, 1), (3, 2)])
    link_got = swap_cores(precision_link)
    core_own = swap_cores(precision_diag)
    core_crossed = swap_cores(crossed)
    gathered = (precision_diag, crossed, core_own, core_crossed)
    always = ids(time_id >= 0)
    (strip,) = run(strip_kernel, always, (precision_link, link_got), ((2, *tile),))
    strip_far = swap_chips(strip)
    w, sums_high, diag_low = run(factor_first_kernel, always, gathered, (full, line, blocks))
    sums_low = jnp.ones(line, F32)
    y, gram = run(panel_first_kernel, always, (w, strip, strip_far), (full, blocks), (full,))
    near = tm_cores(
        gram,
        [(2 * t + 1, 2 * t + 3) for t in range(groups - 1)] + [(2 * t, 2 * t) for t in range(groups)],
    )
    other = swap_cores(y)
    far = swap_cores(near)
    (link_new,) = run(link_kernel, ids(time_id % 2 == row_id), (other, y), (full,), (full,), lazy=2, out=ANY)
    x = tm_cores(
        link_new,
        [(2 * t, 2 * t + 2) for t in range(0, groups, 2)]
        + [(2 * t + 1, 2 * t + 1) for t in range(1, groups, 2)],
    )
    edges = ()
    for level in range(1, LEVELS):
        stride = 2 ** (level - 1)
        position = time_id // stride
        active = (position % 2 == 1) & (time_id % stride == 0)
        now = ids(active)
        diag_low, w, sums_low = run(
            factor_kernel,
            now,
            (diag_low, near, far, sums_low),
            (blocks, full, line),
            lazy=3,
            flops=2 * 10**9,
        )
        y, gram, *edges = run(panel_kernel, now, (w, x, *edges), (full, blocks, tile, tile))
        senders = range(stride, groups, 2 * stride)
        back = [(2 * t, 2 * (t - stride)) for t in senders]
        ahead = [(2 * t + 1, 2 * (t + stride) + 1) for t in senders if t + stride < groups]
        near = tm_cores(gram, back + ahead)
        other = swap_cores(y)
        far = swap_cores(near)
        if level + 1 < LEVELS:
            odd = position // 2 % 2
            (link_new,) = run(
                link_kernel,
                ids(active & (odd == row_id)),
                (other, y),
                (full,),
                (full,),
                after=(near,) if level == 2 else (far,),
                lazy=2,
                out=ANY,
            )
            x = tm_cores(
                link_new,
                [(2 * t, 2 * (t + stride)) for t in senders[::2]]
                + [(2 * t + 1, 2 * (t - stride) + 1) for t in senders[1::2]],
            )
        else:
            (link_new,) = run(link_last_kernel, now, (other, y), (tile,), lazy=2)
            link_last = lax.ppermute(link_new, "tm", [(t, t - stride) for t in senders])
    remaining = ids(time_id % 2 ** (LEVELS - 1) == 0)
    to_top = lax.ppermute(edges[0], "row", [(1, 0)])
    pivots, logs = run(
        factor_last_kernel,
        remaining,
        (diag_low, near, far, sums_low, sums_high, precision_diag),
        ((2, *tile), (2, size // 4)),
        (blocks, full, line),
        lazy=3,
    )
    (couplings,) = run(
        couplings_kernel, remaining, (link_last, to_top, edges[1], precision_link), ((2, *tile),), after=(logs,)
    )
    return (pivots, couplings, logs)


def solution(mesh):
    in_specs = (P("tm", "row", "col"), P("tm", "row", "col"))
    out_specs = (P("tm", "row", "col"), P("tm", "row", "col"), P("tm", ("row", "col")))
    return jax.shard_map(shards, mesh=mesh, in_specs=in_specs, out_specs=out_specs, check_vma=False)
```
